1024 devices in a mesh: uv: 64 (over z, y_hi), tm: 16 (over x, y_lo, core).
Axes of the slice: x: 4, y: 8 (y_hi: 4, y_lo: 2; y = y_hi * 2 + y_lo), z: 16, core: 2. Of those that a mesh axis runs over, the one named last changes fastest.
Arguments:
- visibility: bfloat16 [3, 64, 256, 8, 128], P(None, 'uv', 'tm'), may hold values from -0.15625 to 0.15625
- coordinate: bfloat16 [3, 64, 256, 2, 128], P(None, 'uv', 'tm'), may hold values from 0 to 64
- block_count: int32 [3, 64, 256], P(None, 'uv', 'tm'), may hold values from 1 to 128
- owner_index: int32 [3, 64, 256, 1], P(None, 'uv', 'tm'), may hold values from 0 to 15; in each aligned block of 16 rows (0 to 15, 16 to 31, ..., all dimensions but the last counted through in order) at most 2 rows name the same one
- subgrid_index: int32 [3, 64, 256], P(None, 'uv', 'tm'), may hold values from 0 to 3
- offsets: int32 [64, 64, 2], P('uv', 'tm'), may hold values from 0 to 31
- station_pair: int32 [64, 64, 2], P('uv', 'tm'), may hold values from 0 to 63
- screens: bfloat16 [64, 64, 8, 1024], P('uv'), may hold values from -3 to 3
- slot_owner: int32 [3], replicated, may hold values from 0 to 63
Outputs:
- gridded: float32 [64, 64, 8, 1024], P('uv', 'tm')
The draws below stay inside these ranges and needn't reach their ends.
Inputs may be any that keep to these rules, and one draw needn't show every extreme that they name: `owner_index`: in each slot, at most 2 of the 16 blocks of one device name the same owner, and that many do on some device.
All inputs are finite; a program needn't handle non-finite values.
Results may differ from the reference program's by a relative error of at most 0.0035.
Values may be sent and summed in bfloat16 or wider, within the bound.
No kernel may reach another device: no remote copies, remote signals or barrier semaphores. Data moves between devices by JAX's collectives and lax.ppermute only.
A program may use at most 32 MiB of HBM per device.

```python
import math
import jax
import jax.numpy as jnp
import numpy as np
from jax import lax

SLOTS = 3
SIDE = 32
PIX = 1024
STN = 64
R = 128
BLK = 16
SUB_DEV = 4
CAP = 2
NBLK = 256
NSUB = 64
N_UV = 64
N_TM = 16


def place_ends(entries, rng, least, top_value):
    spot = [jax.random.randint(jax.random.fold_in(rng, axis), (), 0, length) for axis, length in enumerate(entries.shape)]
    main_axis = entries.shape.index(max(entries.shape))
    beside = spot[:main_axis] + [(spot[main_axis] + 1) % entries.shape[main_axis]] + spot[main_axis + 1:]
    return entries.at[tuple(spot)].set(least).at[tuple(beside)].set(top_value)


def steps_of(stream_key, shape, cuts, low, high):
    def one(position, blocks):
        draws = jax.random.uniform(jax.random.fold_in(jax.random.fold_in(stream_key, 6), position), (blocks,), jnp.float32, low / len(cuts), high / len(cuts))
        return jnp.repeat(jnp.exp(draws), shape[position] // blocks).reshape((-1,) + (1,) * (len(shape) - position - 1))

    loudness = one(*cuts[0])
    for cut in cuts[1:]:
        loudness = loudness * one(*cut)
    return loudness


def deal_out(own_key, own, number, rows, count, top, bound, skew):
    sequence = jax.random.permutation(own_key, count)
    crowded, usual = portions_of(count, rows * top, bound, skew, True), portions_of(count, rows * top, bound, skew, False)
    places = jnp.arange(count)

    def named(tallies, turn):
        used = int((tallies > 0).sum())
        fixed = max(1, used // 4)
        passed = fixed + (places - fixed + turn * (used - fixed)) % max(1, count - fixed)
        return jnp.zeros((count,), jnp.int32).at[sequence[jnp.where(places < fixed, places, passed)]].set(jnp.asarray(tallies, jnp.int32))

    tallies = jnp.where(number % 4 == 0, named(crowded, number // 4), named(usual, number - number // 4 - 1))
    mixed = jax.random.permutation(jax.random.fold_in(own, 3), count)
    giver, receiver = mixed[0:count // 2 * 2:2], mixed[1:count // 2 * 2:2]
    margin = jnp.minimum(tallies[giver] - 1, bound - tallies[receiver]) // 2
    margin = jnp.where((giver == sequence[0]) | (receiver == sequence[0]) | (tallies[receiver] == 0), 0, jnp.maximum(margin, 0))
    passed = jax.random.randint(jax.random.fold_in(own, 4), (count // 2,), 0, 1 << 20) % (margin + 1)
    tallies = tallies.at[giver].add(-passed).at[receiver].add(passed)
    items = jnp.searchsorted(jnp.cumsum(tallies), jnp.arange(rows * top), side="right").astype(jnp.int32)
    table = items.reshape(top, rows).T
    table = table[jax.random.permutation(jax.random.fold_in(own, 1), rows)]
    turn = jax.random.randint(jax.random.fold_in(own, 2), (rows, 1), 0, top)
    return jnp.take_along_axis(table, (jnp.arange(top)[None, :] + turn) % top, axis=1)


def portions_of(amount, total, most, skew, full):
    loads = [(1 << 20) // math.isqrt(standing ** skew) + 1 for standing in range(1, amount + 1)]
    largest = most if full else min(most, max(-(-total // amount), total * loads[0] // sum(loads)))
    least = 1 if total - largest >= amount - 1 else 0
    counts, spare = [largest] + [least] * (amount - 1), total - largest - least * (amount - 1)
    while spare > 0:
        movable = [i for i in range(1, amount) if counts[i] < largest] or [i for i in range(1, amount) if counts[i] < most]
        pool, budget = sum([loads[i] for i in movable]), spare
        for i in movable:
            addition = min(most - counts[i], max(1, budget * loads[i] // pool), spare)
            counts[i] = counts[i] + addition
            spare = spare - addition
    return np.array(counts)


def scatter_about(rng, extent, deviation, reach, cuts=(), kind=jnp.bfloat16):
    result = deviation * jax.random.normal(rng, extent, jnp.float32)
    if cuts:
        result = result * steps_of(rng, extent, cuts, -0.22, 0.18)
    return jnp.clip(result, -reach, reach).astype(kind)


def setup_inputs(seed: int = 0) -> dict:
    splits = jax.random.split(jax.random.key(seed), 10)
    visibility = scatter_about(splits[0], (SLOTS, N_UV, NBLK, 8, R), ((SUB_DEV / (BLK * R * SLOTS)) ** 0.5), 0.15625, ((1, 64), (2, 16)))
    coordinate = jnp.clip(64.0 * jax.random.uniform(splits[1], (SLOTS, N_UV, NBLK, 2, R), jnp.float32) ** steps_of(splits[1], (SLOTS, N_UV, NBLK, 2, R), ((1, 64), (2, 16)), -0.2, 0.2), 0.0, 64.0).astype(jnp.bfloat16)
    block_count = place_ends(jax.random.randint(splits[2], (SLOTS, N_UV, NBLK), 1, R + 1), jax.random.fold_in(splits[2], 1), 1, R).astype(jnp.int32)
    owner_index_keys = jax.random.split(jax.random.fold_in(splits[3], 1), SLOTS * N_UV * NBLK // BLK)
    owner_index_turns = jax.random.permutation(jax.random.fold_in(splits[3], 3), SLOTS * N_UV * NBLK // BLK)
    owner_index = jax.vmap(lambda own, number: deal_out(jax.random.fold_in(splits[3], 2), own, number, BLK, N_TM, 1, CAP, 2))(owner_index_keys, owner_index_turns).reshape((SLOTS, N_UV, NBLK, 1))
    subgrid_index = place_ends(jax.random.randint(splits[4], (SLOTS, N_UV, NBLK), 0, SUB_DEV), jax.random.fold_in(splits[4], 1), 0, SUB_DEV - 1).astype(jnp.int32)
    offsets = place_ends(jax.random.randint(splits[5], (N_UV, NSUB, 2), 0, SIDE), jax.random.fold_in(splits[5], 1), 0, SIDE - 1).astype(jnp.int32)
    station_pair = place_ends(jax.random.randint(splits[6], (N_UV, NSUB, 2), 0, STN), jax.random.fold_in(splits[6], 1), 0, STN - 1).astype(jnp.int32)
    screens = scatter_about(splits[7], (N_UV, STN, 8, PIX), 0.5, 3.0, ((0, 64),))
    slot_owner = jax.random.randint(splits[8], (SLOTS,), 0, N_UV).astype(jnp.int32)
    return dict(visibility=visibility, coordinate=coordinate, block_count=block_count, owner_index=owner_index, subgrid_index=subgrid_index, offsets=offsets, station_pair=station_pair, screens=screens, slot_owner=slot_owner)


full_turn = 2.0 * math.pi


def grid_terms(packed, shift_u, shift_v):
    centred = jnp.arange(SIDE, dtype=jnp.float32) - jnp.float32(SIDE // 2)
    values = packed[:, 0:8, :].astype(jnp.float32)
    delta_u = packed[:, 8, :].astype(jnp.float32) - shift_u[:, None]
    delta_v = packed[:, 9, :].astype(jnp.float32) - shift_v[:, None]
    angle_u = (full_turn / SIDE) * centred[None, :, None] * delta_u[:, None, :]
    angle_v = (full_turn / SIDE) * centred[None, :, None] * delta_v[:, None, :]
    left_table = jnp.concatenate([jnp.cos(angle_u), jnp.sin(angle_u)], axis=1).astype(jnp.bfloat16)
    cos_v = jnp.cos(angle_v)[:, None, :, :]
    sin_v = jnp.sin(angle_v)[:, None, :, :]
    real_vis = values[:, 0:4, None, :]
    imag_vis = values[:, 4:8, None, :]
    real_w = real_vis * cos_v - imag_vis * sin_v
    imag_w = real_vis * sin_v + imag_vis * cos_v
    right_table = jnp.concatenate([real_w, imag_w], axis=1)
    right_table = right_table.reshape(packed.shape[0], 8 * SIDE, packed.shape[2]).astype(jnp.bfloat16)
    return jnp.einsum("blr,bkr->blk", left_table.astype(jnp.float32), right_table.astype(jnp.float32))


def arrange(summed):
    count_sub = summed.shape[0]
    upper = summed[:, :SIDE, :]
    lower = summed[:, SIDE:, :]
    half_cols = 4 * SIDE
    real_part = upper[:, :, :half_cols] - lower[:, :, half_cols:]
    imag_part = upper[:, :, half_cols:] + lower[:, :, :half_cols]
    stacked = jnp.stack([real_part, imag_part], axis=1)
    stacked = stacked.reshape(count_sub, 2, SIDE, 4, SIDE).transpose(0, 1, 3, 2, 4)
    return stacked.reshape(count_sub, 8, SIDE * SIDE)


def matrix_product(first, second, conjugate_right):
    real_list = []
    imag_list = []
    for i in range(2):
        for j in range(2):
            real_sum = jnp.zeros_like(first[:, 0, :])
            imag_sum = jnp.zeros_like(first[:, 0, :])
            for k in range(2):
                left_real = first[:, 2 * i + k, :]
                left_imag = first[:, 4 + 2 * i + k, :]
                if conjugate_right:
                    right_real = second[:, 2 * j + k, :]
                    right_imag = -second[:, 4 + 2 * j + k, :]
                else:
                    right_real = second[:, 2 * k + j, :]
                    right_imag = second[:, 4 + 2 * k + j, :]
                real_sum = real_sum + left_real * right_real - left_imag * right_imag
                imag_sum = imag_sum + left_real * right_imag + left_imag * right_real
            real_list.append(real_sum)
            imag_list.append(imag_sum)
    return jnp.stack(real_list + imag_list, axis=1)


def apply_screens(subgrid_image, jones_table, pairs):
    first = jnp.take(jones_table, pairs[:, 0], axis=0).astype(jnp.float32)
    second = jnp.take(jones_table, pairs[:, 1], axis=0).astype(jnp.float32)
    return matrix_product(matrix_product(first, subgrid_image, False), second, True)


def reference(visibility, coordinate, block_count, owner_index, subgrid_index, offsets, station_pair, screens, slot_owner):
    accumulated = jnp.zeros((N_UV, NSUB, 8, PIX), jnp.float32)
    live_rows = jnp.arange(R)[None, None, None, :] < block_count[..., None]
    for slot_id in range(SLOTS):
        jones_table = jnp.take(screens, slot_owner[slot_id], axis=0)

        def one_group(items):
            samples, positions, is_live, owner_row, local_row, shift_rows, pairs = items
            samples = jnp.where(is_live[:, None, :], samples, jnp.zeros((), jnp.bfloat16))
            packed = jnp.concatenate([samples, positions], axis=1)
            target = (owner_row * SUB_DEV + local_row).astype(jnp.int32)
            anchor = jnp.take(shift_rows, target, axis=0).astype(jnp.float32)
            block_terms = grid_terms(packed, anchor[:, 0], anchor[:, 1])
            summed = jax.ops.segment_sum(block_terms, target, num_segments=NSUB)
            return apply_screens(arrange(summed), jones_table, pairs)

        accumulated = accumulated + lax.map(one_group, (visibility[slot_id], coordinate[slot_id], live_rows[slot_id], owner_index[slot_id, :, :, 0], subgrid_index[slot_id], offsets, station_pair))
    return accumulated
```

```python
import jax
import jax.numpy as jnp
from jax import lax
from jax.experimental import pallas as pl
from jax.experimental.pallas import tpu as pltpu
from jax.sharding import PartitionSpec as P

SLOTS = 3
SIDE = 32
BLOCKS = 16
PEERS = 16
CAP = 2
SUBS = 4
STATIONS = 64
PER = SLOTS * CAP
Z_PART = 16
Y_PART = 4
ST_PIECE = STATIONS // Z_PART
REQS = 2 * SUBS
LANES = 128
F32 = jnp.float32
BF16 = jnp.bfloat16

OWNER = 0
SUB = OWNER + SLOTS * BLOCKS
COUNT = SUB + SLOTS * BLOCKS
PAIRS = COUNT + SLOTS * BLOCKS
ROOTS = PAIRS + REQS
OFFS = ROOTS + SLOTS
META = 16

COS_POLY = (1.0, -19.73920440673828, 64.93911743164062, -85.45014190673828, 60.167633056640625,
            -25.967601776123047, 6.528658866882324)
SIN_POLY = (6.283185005187988, -41.341590881347656, 81.59994506835938, -76.6144790649414,
            41.34288787841797, -12.471244812011719)


def smem():
    return pl.BlockSpec(memory_space=pltpu.SMEM)


def vmem():
    return pl.BlockSpec(memory_space=pltpu.VMEM)


def horner(x, poly):
    total = jnp.full_like(x, poly[-1])
    for coefficient in poly[-2::-1]:
        total = total * x + coefficient
    return total


def cis(turns):
    part = turns - jnp.floor(turns + 0.5)
    square = part * part
    return horner(square, COS_POLY), horner(square, SIN_POLY) * part


def times(a, b):
    return a[0] * b[0] - a[1] * b[1], a[0] * b[1] + a[1] * b[0]


def pack_kernel(ints, vis_ref, coord_ref, out_ref, taken):
    lane = lax.broadcasted_iota(jnp.int32, (1, LANES), 1)
    pairs = jnp.zeros((1, LANES), F32)
    for j in range(REQS):
        pairs = jnp.where(lane == META // 2 + j, ints[PAIRS + j].astype(F32), pairs)
    empty = jnp.concatenate([jnp.zeros((10, LANES), F32), pairs, jnp.zeros((5, LANES), F32)], axis=0)
    empty = empty.astype(BF16)

    @pl.loop(0, PEERS)
    def _(o):
        for k in range(PER):
            out_ref[o, k] = empty

    for slot in range(SLOTS):
        for o in range(PEERS):
            taken[o] = 0

        @pl.loop(0, BLOCKS)
        def _(i):
            spot = slot * BLOCKS + i
            owner = ints[OWNER + spot]
            rank = taken[owner]
            taken[owner] = rank + 1
            values = vis_ref[slot, 0, i].astype(F32)
            values = jnp.where(lane < ints[COUNT + spot], values, 0.0)
            meta = jnp.where(lane == 0, ints[SUB + spot].astype(F32), jnp.where(lane == 1, 1.0, pairs))
            rows = jnp.concatenate(
                [values, coord_ref[slot, 0, i].astype(F32), meta, jnp.zeros((5, LANES), F32)], axis=0
            )
            out_ref[owner, slot * CAP + rank] = rows.astype(BF16)


def pack(ints, visibility, coordinate, **kw):
    return pl.pallas_call(
        pack_kernel,
        out_shape=jax.ShapeDtypeStruct((PEERS, PER, 16, LANES), BF16),
        in_specs=[smem(), vmem(), vmem()],
        out_specs=vmem(),
        scratch_shapes=[pltpu.SMEM((PEERS,), jnp.int32)],
        name="pack_blocks",
        cost_estimate=pl.CostEstimate(flops=2000000, bytes_accessed=600000, transcendentals=0),
        **kw,
    )(ints, visibility, coordinate)


def block_transpose(rows):
    lane = lax.broadcasted_iota(jnp.int32, (8, LANES), 1)
    rows = list(rows)
    for bit in range(2):
        step = SIDE << bit
        upper = (lane & step) != 0
        for low in range(4):
            if low >> bit & 1:
                continue
            high = low | 1 << bit
            x, y = rows[low], rows[high]
            rows[low] = jnp.where(upper, pltpu.roll(y, step, 1), x)
            rows[high] = jnp.where(upper, y, pltpu.roll(x, LANES - step, 1))
    return rows


BATCH = 4


def grid_kernel(meta, ints, rows_ref, x_ref, acc, order, bucket):
    acc[...] = jnp.zeros_like(acc)

    def gather(t, carry):
        count, spare = carry
        for k in range(PER):
            b = t * PER + k
            sub = meta[b * META]
            live = meta[b * META + 1]
            order[count] = b
            bucket[count] = (k // CAP) * SUBS + sub
            spare = jnp.where(live == 0, b, spare)
            count = count + live
        return count, spare

    count, spare = lax.fori_loop(0, PEERS, gather, (jnp.int32(0), jnp.int32(0)))
    for j in range(BATCH):
        order[count + j] = spare
        bucket[count + j] = 0

    sublane = lax.broadcasted_iota(jnp.int32, (8, LANES), 0).astype(F32)
    seed_l = (sublane * 4.0 - 16.0) * (1.0 / SIDE)
    seed_m = (sublane - 16.0) * (1.0 / SIDE)

    @pl.loop(0, (count + (BATCH - 1)) // BATCH)
    def _(step):
        for j in range(BATCH):
            b = order[step * BATCH + j]
            key = bucket[step * BATCH + j]
            sub = key % SUBS
            tile = rows_ref[b].astype(F32)
            du = tile[8:9, :] - ints[OFFS + 2 * sub].astype(F32)
            dv = tile[9:10, :] - ints[OFFS + 2 * sub + 1].astype(F32)
            du = jnp.broadcast_to(du, (8, LANES))
            dv = jnp.broadcast_to(dv, (8, LANES))
            turn_l = cis(du * (1.0 / SIDE))
            turn_m = cis(dv * (8.0 / SIDE))
            current = cis(du * seed_l)
            cos_rows, sin_rows = [current[0]], [current[1]]
            for _ in range(3):
                current = times(current, turn_l)
                cos_rows.append(current[0])
                sin_rows.append(current[1])
            left = jnp.concatenate(cos_rows + sin_rows, axis=0).astype(BF16)
            phase = [cis(dv * seed_m)]
            for _ in range(3):
                phase.append(times(phase[-1], turn_m))
            real_rows, imag_rows = [], []
            for p in range(4):
                vis = tile[p:p + 1, :], tile[4 + p:5 + p, :]
                for m in range(4):
                    real, imag = times(vis, phase[m])
                    real_rows.append(real)
                    imag_rows.append(imag)
            right = jnp.concatenate(real_rows + imag_rows, axis=0).astype(BF16)
            acc[key] += lax.dot_general(
                left, right, (((1,), (1,)), ((), ())), preferred_element_type=F32
            )

    @pl.loop(0, SLOTS * SUBS)
    def _(key):
        upper = acc[key, 0:SIDE, :]
        lower = acc[key, SIDE:2 * SIDE, :]
        real = upper[:, :LANES] - lower[:, LANES:]
        imag = upper[:, LANES:] + lower[:, :LANES]
        for part, image in enumerate((real, imag)):
            for p, plane in enumerate(block_transpose([image[8 * b:8 * b + 8] for b in range(4)])):
                x_ref[key, 4 * part + p] = plane


def grid_blocks(meta, ints, rows, **kw):
    return pl.pallas_call(
        grid_kernel,
        out_shape=jax.ShapeDtypeStruct((SLOTS * SUBS, 8, 8, LANES), F32),
        in_specs=[smem(), smem(), vmem()],
        out_specs=vmem(),
        scratch_shapes=[
            pltpu.VMEM((SLOTS * SUBS, 2 * SIDE, 8 * SIDE), F32),
            pltpu.SMEM((PEERS * PER + BATCH,), jnp.int32),
            pltpu.SMEM((PEERS * PER + BATCH,), jnp.int32),
        ],
        name="grid_blocks",
        cost_estimate=pl.CostEstimate(flops=800000000, bytes_accessed=800000, transcendentals=0),
        **kw,
    )(meta, ints, rows)


def pick_z_kernel(ints, in_ref, out_ref):
    for s in range(SLOTS):
        piece = in_ref[ints[ROOTS + s] // Y_PART]
        for y in range(Y_PART):
            out_ref[y, s] = piece


def pick_z(ints, pieces, **kw):
    return pl.pallas_call(
        pick_z_kernel,
        out_shape=jax.ShapeDtypeStruct((Y_PART, SLOTS, 16, LANES), BF16),
        in_specs=[smem(), vmem()],
        out_specs=vmem(),
        name="pick_along_z",
        **kw,
    )(ints, pieces)


def pick_y_kernel(ints, in_ref, out_ref):
    pieces = [in_ref[ints[ROOTS + s] % Y_PART, s].astype(F32) for s in range(SLOTS)]
    rows = jnp.concatenate(
        [pieces[s][4 * i:4 * i + 4] for i in range(ST_PIECE) for s in range(SLOTS)], axis=0
    ).astype(BF16)
    for z in range(Z_PART):
        out_ref[z] = rows


def pick_y(ints, pieces, **kw):
    return pl.pallas_call(
        pick_y_kernel,
        out_shape=jax.ShapeDtypeStruct((Z_PART, ST_PIECE * SLOTS * 4, LANES), BF16),
        in_specs=[smem(), vmem()],
        out_specs=vmem(),
        name="pick_along_y",
        **kw,
    )(ints, pieces)


ROWS_ST = SLOTS * 4


def asked_kernel(meta, in_ref, out_ref, table, stage):
    for z in range(Z_PART):
        wide = in_ref[z].astype(F32)
        for i in range(ST_PIECE):
            table[z * ST_PIECE + i, 0:ROWS_ST, :] = wide[ROWS_ST * i:ROWS_ST * (i + 1)]

    @pl.loop(0, PEERS)
    def _(t):
        for r in range(REQS):
            station = meta[t * (PER * META) + META // 2 + r]
            stage[ROWS_ST * r:ROWS_ST * (r + 1), :] = table[station, 0:ROWS_ST, :]
        out_ref[t] = stage[...].astype(BF16)


def asked(meta, pieces, **kw):
    return pl.pallas_call(
        asked_kernel,
        out_shape=jax.ShapeDtypeStruct((PEERS, REQS * ROWS_ST, LANES), BF16),
        in_specs=[smem(), vmem()],
        out_specs=vmem(),
        scratch_shapes=[
            pltpu.VMEM((STATIONS, 16, LANES), F32),
            pltpu.VMEM((REQS * ROWS_ST, LANES), F32),
        ],
        name="asked_stations",
        cost_estimate=pl.CostEstimate(flops=1000000, bytes_accessed=600000, transcendentals=0),
        **kw,
    )(meta, pieces)


def screen_kernel(x_ref, in_ref, out_ref, wide, tmp):
    rows = REQS * ROWS_ST
    for t in range(PEERS):
        wide[rows * t:rows * (t + 1), :] = in_ref[t].astype(F32)

    def entry(request, slot, p, half):
        start = half * rows + request * ROWS_ST + slot * 4 + p
        return wide[pl.ds(start, 8, stride=2 * rows), :]

    def product(first, second):
        result = []
        for i in range(2):
            for j in range(2):
                one = times(first[2 * i], second[j])
                two = times(first[2 * i + 1], second[2 + j])
                result.append((one[0] + two[0], one[1] + two[1]))
        return result

    for sub in range(SUBS):
        total = None
        for slot in range(SLOTS):
            first = [(entry(2 * sub, slot, p, 0), entry(2 * sub, slot, p, 1)) for p in range(4)]
            second = [(entry(2 * sub + 1, slot, p, 0), -entry(2 * sub + 1, slot, p, 1)) for p in (0, 2, 1, 3)]
            key = slot * SUBS + sub
            image = [(x_ref[key, p], x_ref[key, 4 + p]) for p in range(4)]
            part = product(product(first, image), second)
            if total is None:
                total = part
            else:
                total = [(a[0] + b[0], a[1] + b[1]) for a, b in zip(total, part)]
        for p in range(4):
            tmp[8 * p:8 * p + 8, :] = total[p][0]
            tmp[32 + 8 * p:40 + 8 * p, :] = total[p][1]
        for a in range(8):
            out_ref[0, sub, :, LANES * a:LANES * (a + 1)] = tmp[pl.ds(a, 8, stride=8), :]


def screen_product(x, screens, **kw):
    return pl.pallas_call(
        screen_kernel,
        out_shape=jax.ShapeDtypeStruct((1, SUBS, 8, SIDE * SIDE), F32),
        in_specs=[vmem(), vmem()],
        out_specs=vmem(),
        scratch_shapes=[
            pltpu.VMEM((PEERS * REQS * ROWS_ST, LANES), F32),
            pltpu.VMEM((64, LANES), F32),
        ],
        name="screen_product",
        cost_estimate=pl.CostEstimate(flops=3000000, bytes_accessed=1000000, transcendentals=0),
        **kw,
    )(x, screens)


def pack_ints(block_count, owner_index, subgrid_index, offsets, station_pair, slot_owner):
    return jnp.concatenate([
        owner_index.reshape(-1), subgrid_index.reshape(-1), block_count.reshape(-1),
        station_pair.reshape(-1), slot_owner, offsets.reshape(-1),
    ])


def chunk_of(screens, t):
    part = lax.dynamic_slice(screens[0], (0, 4 * (t % 2), LANES * (t // 2)), (STATIONS, 4, LANES))
    return part.reshape(Z_PART, ST_PIECE * 4, LANES)


def meta_of(arrived):
    return arrived[:, :, 10, :META].astype(jnp.int32).reshape(-1)


def on_device(visibility, coordinate, block_count, owner_index, subgrid_index, offsets,
              station_pair, screens, slot_owner):
    z_groups = [[z * Y_PART + y for z in range(Z_PART)] for y in range(Y_PART)]
    y_groups = [[z * Y_PART + y for y in range(Y_PART)] for z in range(Z_PART)]

    def exchange(array, axis, groups=None):
        return lax.all_to_all(array, axis, 0, 0, axis_index_groups=groups, tiled=True)

    ints = pack_ints(block_count, owner_index, subgrid_index, offsets, station_pair, slot_owner)
    sent = pack(ints, visibility, coordinate)
    arrived = exchange(sent, "tm")
    meta = meta_of(arrived)
    pieces = exchange(chunk_of(screens, lax.axis_index("tm")), "uv", z_groups)
    pieces = exchange(pick_z(ints, pieces), "uv", y_groups)
    pieces = exchange(pick_y(ints, pieces), "uv", z_groups)
    x = grid_blocks(meta, ints, arrived.reshape(PEERS * PER, 16, LANES))
    wanted = exchange(asked(meta, pieces), "tm")
    return screen_product(x, wanted)


def solution(mesh):
    placed = (
        P(None, "uv", "tm", None, None),
        P(None, "uv", "tm", None, None),
        P(None, "uv", "tm"),
        P(None, "uv", "tm", None),
        P(None, "uv", "tm"),
        P("uv", "tm", None),
        P("uv", "tm", None),
        P("uv", None, None, None),
        P(),
    )
    return jax.shard_map(
        on_device, mesh=mesh, in_specs=placed, out_specs=P("uv", "tm", None, None), check_vma=False
    )
```

```python
import jax
import jax.numpy as jnp
from jax import lax
from jax.experimental import pallas as pl
from jax.experimental.pallas import tpu as pltpu
from jax.sharding import PartitionSpec as P

SLOTS = 3
SIDE = 32
BLOCKS = 16
PEERS = 16
CAP = 2
SUBS = 4
STATIONS = 64
PER = SLOTS * CAP
Z_PART = 16
Y_PART = 4
NDEV = Z_PART * Y_PART
ST_PIECE = STATIONS // Z_PART
REQS = 2 * SUBS
LANES = 128
F32 = jnp.float32
BF16 = jnp.bfloat16

OWNER = 0
SUB = OWNER + SLOTS * BLOCKS
COUNT = SUB + SLOTS * BLOCKS
PAIRS = COUNT + SLOTS * BLOCKS
ROOTS = PAIRS + REQS
ME = ROOTS + SLOTS
OFFS = ME + 1
META = 16

COS_POLY = (1.0, -19.73920440673828, 64.93911743164062, -85.45014190673828, 60.167633056640625,
            -25.967601776123047, 6.528658866882324)
SIN_POLY = (6.283185005187988, -41.341590881347656, 81.59994506835938, -76.6144790649414,
            41.34288787841797, -12.471244812011719)


def smem():
    return pl.BlockSpec(memory_space=pltpu.SMEM)


def vmem():
    return pl.BlockSpec(memory_space=pltpu.VMEM)


def room():
    return pltpu.CompilerParams(vmem_limit_bytes=8 * 1024 * 1024)


def horner(x, poly):
    total = jnp.full_like(x, poly[-1])
    for coefficient in poly[-2::-1]:
        total = total * x + coefficient
    return total


def cis(turns):
    part = turns - jnp.floor(turns + 0.5)
    square = part * part
    return horner(square, COS_POLY), horner(square, SIN_POLY) * part


def times(a, b):
    return a[0] * b[0] - a[1] * b[1], a[0] * b[1] + a[1] * b[0]


def pack_kernel(ints, vis_ref, coord_ref, out_ref, taken):
    lane = lax.broadcasted_iota(jnp.int32, (1, LANES), 1)
    pairs = jnp.zeros((1, LANES), F32)
    for j in range(REQS):
        pairs = jnp.where(lane == META // 2 + j, ints[PAIRS + j].astype(F32), pairs)
    empty = jnp.concatenate([jnp.zeros((10, LANES), F32), pairs, jnp.zeros((5, LANES), F32)], axis=0)
    empty = empty.astype(BF16)

    @pl.loop(0, PEERS)
    def _(o):
        for k in range(PER):
            out_ref[o, k] = empty

    for slot in range(SLOTS):
        for o in range(PEERS):
            taken[o] = 0

        @pl.loop(0, BLOCKS)
        def _(i):
            spot = slot * BLOCKS + i
            owner = ints[OWNER + spot]
            rank = taken[owner]
            taken[owner] = rank + 1
            values = vis_ref[slot, 0, i].astype(F32)
            values = jnp.where(lane < ints[COUNT + spot], values, 0.0)
            meta = jnp.where(lane == 0, ints[SUB + spot].astype(F32), jnp.where(lane == 1, 1.0, pairs))
            rows = jnp.concatenate(
                [values, coord_ref[slot, 0, i].astype(F32), meta, jnp.zeros((5, LANES), F32)], axis=0
            )
            out_ref[owner, slot * CAP + rank] = rows.astype(BF16)


def pack(ints, visibility, coordinate, **kw):
    return pl.pallas_call(
        pack_kernel,
        out_shape=jax.ShapeDtypeStruct((PEERS, PER, 16, LANES), BF16),
        in_specs=[smem(), vmem(), vmem()],
        out_specs=vmem(),
        scratch_shapes=[pltpu.SMEM((PEERS,), jnp.int32)],
        name="pack_blocks",
        cost_estimate=pl.CostEstimate(flops=2000000, bytes_accessed=600000, transcendentals=0),
        compiler_params=room(),
        **kw,
    )(ints, visibility, coordinate)


def block_transpose(rows):
    lane = lax.broadcasted_iota(jnp.int32, (8, LANES), 1)
    rows = list(rows)
    for bit in range(2):
        step = SIDE << bit
        upper = (lane & step) != 0
        for low in range(4):
            if low >> bit & 1:
                continue
            high = low | 1 << bit
            x, y = rows[low], rows[high]
            rows[low] = jnp.where(upper, pltpu.roll(y, step, 1), x)
            rows[high] = jnp.where(upper, y, pltpu.roll(x, LANES - step, 1))
    return rows


BATCH = 4


def grid_kernel(meta, ints, rows_ref, x_ref, acc, order, bucket):
    acc[...] = jnp.zeros_like(acc)

    def gather(t, carry):
        count, spare = carry
        for k in range(PER):
            b = t * PER + k
            sub = meta[b * META]
            live = meta[b * META + 1]
            order[count] = b
            bucket[count] = (k // CAP) * SUBS + sub
            spare = jnp.where(live == 0, b, spare)
            count = count + live
        return count, spare

    count, spare = lax.fori_loop(0, PEERS, gather, (jnp.int32(0), jnp.int32(0)))
    for j in range(BATCH):
        order[count + j] = spare
        bucket[count + j] = 0

    sublane = lax.broadcasted_iota(jnp.int32, (8, LANES), 0).astype(F32)
    seed_l = (sublane * 4.0 - 16.0) * (1.0 / SIDE)
    seed_m = (sublane - 16.0) * (1.0 / SIDE)

    @pl.loop(0, (count + (BATCH - 1)) // BATCH)
    def _(step):
        for j in range(BATCH):
            b = order[step * BATCH + j]
            key = bucket[step * BATCH + j]
            sub = key % SUBS
            tile = rows_ref[b].astype(F32)
            du = tile[8:9, :] - ints[OFFS + 2 * sub].astype(F32)
            dv = tile[9:10, :] - ints[OFFS + 2 * sub + 1].astype(F32)
            du = jnp.broadcast_to(du, (8, LANES))
            dv = jnp.broadcast_to(dv, (8, LANES))
            turn_l = cis(du * (1.0 / SIDE))
            turn_m = cis(dv * (8.0 / SIDE))
            current = cis(du * seed_l)
            cos_rows, sin_rows = [current[0]], [current[1]]
            for _ in range(3):
                current = times(current, turn_l)
                cos_rows.append(current[0])
                sin_rows.append(current[1])
            left = jnp.concatenate(cos_rows + sin_rows, axis=0).astype(BF16)
            phase = [cis(dv * seed_m)]
            for _ in range(3):
                phase.append(times(phase[-1], turn_m))
            real_rows, imag_rows = [], []
            for p in range(4):
                vis = tile[p:p + 1, :], tile[4 + p:5 + p, :]
                for m in range(4):
                    real, imag = times(vis, phase[m])
                    real_rows.append(real)
                    imag_rows.append(imag)
            right = jnp.concatenate(real_rows + imag_rows, axis=0).astype(BF16)
            acc[key] += lax.dot_general(
                left, right, (((1,), (1,)), ((), ())), preferred_element_type=F32
            )

    @pl.loop(0, SLOTS * SUBS)
    def _(key):
        upper = acc[key, 0:SIDE, :]
        lower = acc[key, SIDE:2 * SIDE, :]
        real = upper[:, :LANES] - lower[:, LANES:]
        imag = upper[:, LANES:] + lower[:, :LANES]
        for part, image in enumerate((real, imag)):
            for p, plane in enumerate(block_transpose([image[8 * b:8 * b + 8] for b in range(4)])):
                x_ref[key, 4 * part + p] = plane


def grid_blocks(meta, ints, rows, **kw):
    return pl.pallas_call(
        grid_kernel,
        out_shape=jax.ShapeDtypeStruct((SLOTS * SUBS, 8, 8, LANES), F32),
        in_specs=[smem(), smem(), vmem()],
        out_specs=vmem(),
        scratch_shapes=[
            pltpu.VMEM((SLOTS * SUBS, 2 * SIDE, 8 * SIDE), F32),
            pltpu.SMEM((PEERS * PER + BATCH,), jnp.int32),
            pltpu.SMEM((PEERS * PER + BATCH,), jnp.int32),
        ],
        name="grid_blocks",
        cost_estimate=pl.CostEstimate(flops=800000000, bytes_accessed=800000, transcendentals=0),
        compiler_params=room(),
        **kw,
    )(meta, ints, rows)


def pick_z_kernel(ints, in_ref, out_ref):
    for s in range(SLOTS):
        out_ref[s] = in_ref[ints[ROOTS + s] // Y_PART]


def pick_z(ints, pieces, **kw):
    return pl.pallas_call(
        pick_z_kernel,
        out_shape=jax.ShapeDtypeStruct((SLOTS, 16, LANES), BF16),
        in_specs=[smem(), vmem()],
        out_specs=vmem(),
        name="pick_along_z",
        compiler_params=room(),
        **kw,
    )(ints, pieces)


def pick_y_kernel(ints, *refs):
    out_ref = refs[Y_PART]
    pieces = []
    for s in range(SLOTS):
        shift = (ints[ME] - ints[ROOTS + s] + NDEV) % Y_PART
        piece = refs[0][s].astype(F32)
        for y in range(1, Y_PART):
            piece = jnp.where(shift == y, refs[y][s].astype(F32), piece)
        pieces.append(piece)
    rows = jnp.concatenate(
        [pieces[s][4 * i:4 * i + 4] for i in range(ST_PIECE) for s in range(SLOTS)], axis=0
    ).astype(BF16)
    for z in range(Z_PART):
        out_ref[z] = rows


def pick_y(ints, pieces, **kw):
    return pl.pallas_call(
        pick_y_kernel,
        out_shape=jax.ShapeDtypeStruct((Z_PART, ST_PIECE * SLOTS * 4, LANES), BF16),
        in_specs=[smem()] + [vmem()] * Y_PART,
        out_specs=vmem(),
        name="pick_along_y",
        compiler_params=room(),
        **kw,
    )(ints, *pieces)


ROWS_ST = SLOTS * 4


def asked_kernel(meta, in_ref, out_ref, table, stage):
    for z in range(Z_PART):
        wide = in_ref[z].astype(F32)
        for i in range(ST_PIECE):
            table[z * ST_PIECE + i, 0:ROWS_ST, :] = wide[ROWS_ST * i:ROWS_ST * (i + 1)]

    @pl.loop(0, PEERS)
    def _(t):
        for r in range(REQS):
            station = meta[t * (PER * META) + META // 2 + r]
            stage[ROWS_ST * r:ROWS_ST * (r + 1), :] = table[station, 0:ROWS_ST, :]
        out_ref[t] = stage[...].astype(BF16)


def asked(meta, pieces, **kw):
    return pl.pallas_call(
        asked_kernel,
        out_shape=jax.ShapeDtypeStruct((PEERS, REQS * ROWS_ST, LANES), BF16),
        in_specs=[smem(), vmem()],
        out_specs=vmem(),
        scratch_shapes=[
            pltpu.VMEM((STATIONS, 16, LANES), F32),
            pltpu.VMEM((REQS * ROWS_ST, LANES), F32),
        ],
        name="asked_stations",
        cost_estimate=pl.CostEstimate(flops=1000000, bytes_accessed=600000, transcendentals=0),
        compiler_params=room(),
        **kw,
    )(meta, pieces)


def screen_kernel(x_ref, in_ref, out_ref, wide, tmp):
    rows = REQS * ROWS_ST
    for t in range(PEERS):
        wide[rows * t:rows * (t + 1), :] = in_ref[t].astype(F32)

    def entry(request, slot, p, half):
        start = half * rows + request * ROWS_ST + slot * 4 + p
        return wide[pl.ds(start, 8, stride=2 * rows), :]

    def product(first, second):
        result = []
        for i in range(2):
            for j in range(2):
                one = times(first[2 * i], second[j])
                two = times(first[2 * i + 1], second[2 + j])
                result.append((one[0] + two[0], one[1] + two[1]))
        return result

    for sub in range(SUBS):
        total = None
        for slot in range(SLOTS):
            first = [(entry(2 * sub, slot, p, 0), entry(2 * sub, slot, p, 1)) for p in range(4)]
            second = [(entry(2 * sub + 1, slot, p, 0), -entry(2 * sub + 1, slot, p, 1)) for p in (0, 2, 1, 3)]
            key = slot * SUBS + sub
            image = [(x_ref[key, p], x_ref[key, 4 + p]) for p in range(4)]
            part = product(product(first, image), second)
            if total is None:
                total = part
            else:
                total = [(a[0] + b[0], a[1] + b[1]) for a, b in zip(total, part)]
        for p in range(4):
            tmp[8 * p:8 * p + 8, :] = total[p][0]
            tmp[32 + 8 * p:40 + 8 * p, :] = total[p][1]
        for a in range(8):
            out_ref[0, sub, :, LANES * a:LANES * (a + 1)] = tmp[pl.ds(a, 8, stride=8), :]


def screen_product(x, screens, **kw):
    return pl.pallas_call(
        screen_kernel,
        out_shape=jax.ShapeDtypeStruct((1, SUBS, 8, SIDE * SIDE), F32),
        in_specs=[vmem(), vmem()],
        out_specs=vmem(),
        scratch_shapes=[
            pltpu.VMEM((PEERS * REQS * ROWS_ST, LANES), F32),
            pltpu.VMEM((64, LANES), F32),
        ],
        name="screen_product",
        cost_estimate=pl.CostEstimate(flops=3000000, bytes_accessed=1000000, transcendentals=0),
        compiler_params=room(),
        **kw,
    )(x, screens)


def pack_ints(block_count, owner_index, subgrid_index, offsets, station_pair, slot_owner, me):
    return jnp.concatenate([
        owner_index.reshape(-1), subgrid_index.reshape(-1), block_count.reshape(-1),
        station_pair.reshape(-1), slot_owner, me.reshape(-1), offsets.reshape(-1),
    ])


def chunk_of(screens, t):
    part = lax.dynamic_slice(screens[0], (0, 4 * (t % 2), LANES * (t // 2)), (STATIONS, 4, LANES))
    return part.reshape(Z_PART, ST_PIECE * 4, LANES)


def meta_of(arrived):
    return arrived[:, :, 10, :META].astype(jnp.int32).reshape(-1)


def on_device(visibility, coordinate, block_count, owner_index, subgrid_index, offsets,
              station_pair, screens, slot_owner):
    z_groups = [[z * Y_PART + y for z in range(Z_PART)] for y in range(Y_PART)]
    y_shifts = [
        [(z * Y_PART + y, z * Y_PART + (y + shift) % Y_PART) for z in range(Z_PART) for y in range(Y_PART)]
        for shift in range(1, Y_PART)
    ]

    def exchange(array, axis, groups=None):
        return lax.all_to_all(array, axis, 0, 0, axis_index_groups=groups, tiled=True)

    ints = pack_ints(block_count, owner_index, subgrid_index, offsets, station_pair, slot_owner,
                     lax.axis_index("uv"))
    sent = pack(ints, visibility, coordinate)
    arrived = exchange(sent, "tm")
    meta = meta_of(arrived)
    pieces = exchange(chunk_of(screens, lax.axis_index("tm")), "uv", z_groups)
    piece = pick_z(ints, pieces)
    pieces = [piece] + [lax.ppermute(piece, "uv", shift) for shift in y_shifts]
    pieces = exchange(pick_y(ints, pieces), "uv", z_groups)
    x = grid_blocks(meta, ints, arrived.reshape(PEERS * PER, 16, LANES))
    wanted = exchange(asked(meta, pieces), "tm")
    return screen_product(x, wanted)


def solution(mesh):
    placed = (
        P(None, "uv", "tm", None, None),
        P(None, "uv", "tm", None, None),
        P(None, "uv", "tm"),
        P(None, "uv", "tm", None),
        P(None, "uv", "tm"),
        P("uv", "tm", None),
        P("uv", "tm", None),
        P("uv", None, None, None),
        P(),
    )
    return jax.shard_map(
        on_device, mesh=mesh, in_specs=placed, out_specs=P("uv", "tm", None, None), check_vma=False
    )
```

```python
import jax
import jax.numpy as jnp
from jax import lax
from jax.experimental import pallas as pl
from jax.experimental.pallas import tpu as pltpu
from jax.sharding import PartitionSpec as P

SLOTS = 3
SIDE = 32
BLOCKS = 16
PEERS = 16
CAP = 2
SUBS = 4
STATIONS = 64
PER = SLOTS * CAP
NEAR = 16
FAR = 4
NDEV = NEAR * FAR
ST_PIECE = STATIONS // NEAR
REQS = 2 * SUBS
LANES = 128
F32 = jnp.float32
BF16 = jnp.bfloat16

OWNER = 0
SUB = OWNER + SLOTS * BLOCKS
COUNT = SUB + SLOTS * BLOCKS
PAIRS = COUNT + SLOTS * BLOCKS
ROOTS = PAIRS + REQS
ME = ROOTS + SLOTS
OFFS = ME + 1
META = 16

COS_POLY = (1.0, -19.73920440673828, 64.93911743164062, -85.45014190673828, 60.167633056640625,
            -25.967601776123047, 6.528658866882324)
SIN_POLY = (6.283185005187988, -41.341590881347656, 81.59994506835938, -76.6144790649414,
            41.34288787841797, -12.471244812011719)


def smem():
    return pl.BlockSpec(memory_space=pltpu.SMEM)


def vmem():
    return pl.BlockSpec(memory_space=pltpu.VMEM)


def room():
    return pltpu.CompilerParams(vmem_limit_bytes=8 * 1024 * 1024)


def horner(x, poly):
    total = jnp.full_like(x, poly[-1])
    for coefficient in poly[-2::-1]:
        total = total * x + coefficient
    return total


def cis(turns):
    part = turns - jnp.floor(turns + 0.5)
    square = part * part
    return horner(square, COS_POLY), horner(square, SIN_POLY) * part


def times(a, b):
    return a[0] * b[0] - a[1] * b[1], a[0] * b[1] + a[1] * b[0]


def pack_kernel(ints, vis_ref, coord_ref, out_ref, taken):
    lane = lax.broadcasted_iota(jnp.int32, (1, LANES), 1)
    pairs = jnp.zeros((1, LANES), F32)
    for j in range(REQS):
        pairs = jnp.where(lane == META // 2 + j, ints[PAIRS + j].astype(F32), pairs)
    empty = jnp.concatenate([jnp.zeros((10, LANES), F32), pairs, jnp.zeros((5, LANES), F32)], axis=0)
    empty = empty.astype(BF16)

    @pl.loop(0, PEERS)
    def _(o):
        for k in range(PER):
            out_ref[o, k] = empty

    for slot in range(SLOTS):
        for o in range(PEERS):
            taken[o] = 0

        @pl.loop(0, BLOCKS)
        def _(i):
            spot = slot * BLOCKS + i
            owner = ints[OWNER + spot]
            rank = taken[owner]
            taken[owner] = rank + 1
            values = vis_ref[slot, 0, i].astype(F32)
            values = jnp.where(lane < ints[COUNT + spot], values, 0.0)
            meta = jnp.where(lane == 0, ints[SUB + spot].astype(F32), jnp.where(lane == 1, 1.0, pairs))
            rows = jnp.concatenate(
                [values, coord_ref[slot, 0, i].astype(F32), meta, jnp.zeros((5, LANES), F32)], axis=0
            )
            out_ref[owner, slot * CAP + rank] = rows.astype(BF16)


def pack(ints, visibility, coordinate, **kw):
    return pl.pallas_call(
        pack_kernel,
        out_shape=jax.ShapeDtypeStruct((PEERS, PER, 16, LANES), BF16),
        in_specs=[smem(), vmem(), vmem()],
        out_specs=vmem(),
        scratch_shapes=[pltpu.SMEM((PEERS,), jnp.int32)],
        name="pack_blocks",
        cost_estimate=pl.CostEstimate(flops=2000000, bytes_accessed=600000, transcendentals=0),
        compiler_params=room(),
        **kw,
    )(ints, visibility, coordinate)


def block_transpose(rows):
    lane = lax.broadcasted_iota(jnp.int32, (8, LANES), 1)
    rows = list(rows)
    for bit in range(2):
        step = SIDE << bit
        upper = (lane & step) != 0
        for low in range(4):
            if low >> bit & 1:
                continue
            high = low | 1 << bit
            x, y = rows[low], rows[high]
            rows[low] = jnp.where(upper, pltpu.roll(y, step, 1), x)
            rows[high] = jnp.where(upper, y, pltpu.roll(x, LANES - step, 1))
    return rows


BATCH = 4


def grid_kernel(meta, ints, rows_ref, x_ref, acc, order, bucket):
    acc[...] = jnp.zeros_like(acc)

    def gather(t, carry):
        count, spare = carry
        for k in range(PER):
            b = t * PER + k
            sub = meta[b * META]
            live = meta[b * META + 1]
            order[count] = b
            bucket[count] = (k // CAP) * SUBS + sub
            spare = jnp.where(live == 0, b, spare)
            count = count + live
        return count, spare

    count, spare = lax.fori_loop(0, PEERS, gather, (jnp.int32(0), jnp.int32(0)))
    for j in range(BATCH):
        order[count + j] = spare
        bucket[count + j] = 0

    sublane = lax.broadcasted_iota(jnp.int32, (8, LANES), 0).astype(F32)
    seed_l = (sublane * 4.0 - 16.0) * (1.0 / SIDE)
    seed_m = (sublane - 16.0) * (1.0 / SIDE)

    @pl.loop(0, (count + (BATCH - 1)) // BATCH)
    def _(step):
        for j in range(BATCH):
            b = order[step * BATCH + j]
            key = bucket[step * BATCH + j]
            sub = key % SUBS
            tile = rows_ref[b].astype(F32)
            du = tile[8:9, :] - ints[OFFS + 2 * sub].astype(F32)
            dv = tile[9:10, :] - ints[OFFS + 2 * sub + 1].astype(F32)
            du = jnp.broadcast_to(du, (8, LANES))
            dv = jnp.broadcast_to(dv, (8, LANES))
            turn_l = cis(du * (1.0 / SIDE))
            turn_m = cis(dv * (8.0 / SIDE))
            current = cis(du * seed_l)
            cos_rows, sin_rows = [current[0]], [current[1]]
            for _ in range(3):
                current = times(current, turn_l)
                cos_rows.append(current[0])
                sin_rows.append(current[1])
            left = jnp.concatenate(cos_rows + sin_rows, axis=0).astype(BF16)
            phase = [cis(dv * seed_m)]
            for _ in range(3):
                phase.append(times(phase[-1], turn_m))
            real_rows, imag_rows = [], []
            for p in range(4):
                vis = tile[p:p + 1, :], tile[4 + p:5 + p, :]
                for m in range(4):
                    real, imag = times(vis, phase[m])
                    real_rows.append(real)
                    imag_rows.append(imag)
            right = jnp.concatenate(real_rows + imag_rows, axis=0).astype(BF16)
            acc[key] += lax.dot_general(
                left, right, (((1,), (1,)), ((), ())), preferred_element_type=F32
            )

    @pl.loop(0, SLOTS * SUBS)
    def _(key):
        upper = acc[key, 0:SIDE, :]
        lower = acc[key, SIDE:2 * SIDE, :]
        real = upper[:, :LANES] - lower[:, LANES:]
        imag = upper[:, LANES:] + lower[:, :LANES]
        for part, image in enumerate((real, imag)):
            for p, plane in enumerate(block_transpose([image[8 * b:8 * b + 8] for b in range(4)])):
                x_ref[key, 4 * part + p] = plane


def grid_blocks(meta, ints, rows, **kw):
    return pl.pallas_call(
        grid_kernel,
        out_shape=jax.ShapeDtypeStruct((SLOTS * SUBS, 8, 8, LANES), F32),
        in_specs=[smem(), smem(), vmem()],
        out_specs=vmem(),
        scratch_shapes=[
            pltpu.VMEM((SLOTS * SUBS, 2 * SIDE, 8 * SIDE), F32),
            pltpu.SMEM((PEERS * PER + BATCH,), jnp.int32),
            pltpu.SMEM((PEERS * PER + BATCH,), jnp.int32),
        ],
        name="grid_blocks",
        cost_estimate=pl.CostEstimate(flops=800000000, bytes_accessed=800000, transcendentals=0),
        compiler_params=room(),
        **kw,
    )(meta, ints, rows)


def pick_near_kernel(ints, in_ref, out_ref):
    for s in range(SLOTS):
        out_ref[s] = in_ref[ints[ROOTS + s] % NEAR]


def pick_near(ints, pieces, **kw):
    return pl.pallas_call(
        pick_near_kernel,
        out_shape=jax.ShapeDtypeStruct((SLOTS, 16, LANES), BF16),
        in_specs=[smem(), vmem()],
        out_specs=vmem(),
        name="pick_near",
        compiler_params=room(),
        **kw,
    )(ints, pieces)


def pick_far_kernel(ints, *refs):
    both_ref, later_ref, out_ref = refs
    pieces = []
    for s in range(SLOTS):
        shift = (ints[ME] // NEAR - ints[ROOTS + s] // NEAR + FAR) % FAR
        k = shift % 2 * SLOTS + s
        piece = jnp.where(shift < 2, both_ref[k].astype(F32), later_ref[k].astype(F32))
        pieces.append(piece)
    rows = jnp.concatenate(
        [pieces[s][4 * i:4 * i + 4] for i in range(ST_PIECE) for s in range(SLOTS)], axis=0
    ).astype(BF16)
    for z in range(NEAR):
        out_ref[z] = rows


def pick_far(ints, pieces, **kw):
    return pl.pallas_call(
        pick_far_kernel,
        out_shape=jax.ShapeDtypeStruct((NEAR, ST_PIECE * SLOTS * 4, LANES), BF16),
        in_specs=[smem(), vmem(), vmem()],
        out_specs=vmem(),
        name="pick_far",
        compiler_params=room(),
        **kw,
    )(ints, *pieces)


ROWS_ST = SLOTS * 4


def asked_kernel(meta, in_ref, out_ref, table, stage):
    for z in range(NEAR):
        wide = in_ref[z].astype(F32)
        for i in range(ST_PIECE):
            table[z * ST_PIECE + i, 0:ROWS_ST, :] = wide[ROWS_ST * i:ROWS_ST * (i + 1)]

    @pl.loop(0, PEERS)
    def _(t):
        for r in range(REQS):
            station = meta[t * (PER * META) + META // 2 + r]
            stage[ROWS_ST * r:ROWS_ST * (r + 1), :] = table[station, 0:ROWS_ST, :]
        out_ref[t] = stage[...].astype(BF16)


def asked(meta, pieces, **kw):
    return pl.pallas_call(
        asked_kernel,
        out_shape=jax.ShapeDtypeStruct((PEERS, REQS * ROWS_ST, LANES), BF16),
        in_specs=[smem(), vmem()],
        out_specs=vmem(),
        scratch_shapes=[
            pltpu.VMEM((STATIONS, 16, LANES), F32),
            pltpu.VMEM((REQS * ROWS_ST, LANES), F32),
        ],
        name="asked_stations",
        cost_estimate=pl.CostEstimate(flops=1000000, bytes_accessed=600000, transcendentals=0),
        compiler_params=room(),
        **kw,
    )(meta, pieces)


def screen_kernel(x_ref, in_ref, out_ref, wide, tmp):
    rows = REQS * ROWS_ST
    for t in range(PEERS):
        wide[rows * t:rows * (t + 1), :] = in_ref[t].astype(F32)

    def entry(request, slot, p, half):
        start = half * rows + request * ROWS_ST + slot * 4 + p
        return wide[pl.ds(start, 8, stride=2 * rows), :]

    def product(first, second):
        result = []
        for i in range(2):
            for j in range(2):
                one = times(first[2 * i], second[j])
                two = times(first[2 * i + 1], second[2 + j])
                result.append((one[0] + two[0], one[1] + two[1]))
        return result

    for sub in range(SUBS):
        total = None
        for slot in range(SLOTS):
            first = [(entry(2 * sub, slot, p, 0), entry(2 * sub, slot, p, 1)) for p in range(4)]
            second = [(entry(2 * sub + 1, slot, p, 0), -entry(2 * sub + 1, slot, p, 1)) for p in (0, 2, 1, 3)]
            key = slot * SUBS + sub
            image = [(x_ref[key, p], x_ref[key, 4 + p]) for p in range(4)]
            part = product(product(first, image), second)
            if total is None:
                total = part
            else:
                total = [(a[0] + b[0], a[1] + b[1]) for a, b in zip(total, part)]
        for p in range(4):
            tmp[8 * p:8 * p + 8, :] = total[p][0]
            tmp[32 + 8 * p:40 + 8 * p, :] = total[p][1]
        for a in range(8):
            out_ref[0, sub, :, LANES * a:LANES * (a + 1)] = tmp[pl.ds(a, 8, stride=8), :]


def screen_product(x, screens, **kw):
    return pl.pallas_call(
        screen_kernel,
        out_shape=jax.ShapeDtypeStruct((1, SUBS, 8, SIDE * SIDE), F32),
        in_specs=[vmem(), vmem()],
        out_specs=vmem(),
        scratch_shapes=[
            pltpu.VMEM((PEERS * REQS * ROWS_ST, LANES), F32),
            pltpu.VMEM((64, LANES), F32),
        ],
        name="screen_product",
        cost_estimate=pl.CostEstimate(flops=3000000, bytes_accessed=1000000, transcendentals=0),
        compiler_params=room(),
        **kw,
    )(x, screens)


def pack_ints(block_count, owner_index, subgrid_index, offsets, station_pair, slot_owner, me):
    return jnp.concatenate([
        owner_index.reshape(-1), subgrid_index.reshape(-1), block_count.reshape(-1),
        station_pair.reshape(-1), slot_owner, me.reshape(-1), offsets.reshape(-1),
    ])


def chunk_of(screens, t):
    part = lax.dynamic_slice(screens[0], (0, 4 * (t % 2), LANES * (t // 2)), (STATIONS, 4, LANES))
    return part.reshape(NEAR, ST_PIECE * 4, LANES)


def meta_of(arrived):
    return arrived[:, :, 10, :META].astype(jnp.int32).reshape(-1)


def on_device(visibility, coordinate, block_count, owner_index, subgrid_index, offsets,
              station_pair, screens, slot_owner):
    near = [[k * NEAR + j for j in range(NEAR)] for k in range(FAR)]
    shifts = [
        [(k * NEAR + j, (k + shift) % FAR * NEAR + j) for k in range(FAR) for j in range(NEAR)]
        for shift in (1, 2)
    ]

    def exchange(array, axis, groups=None):
        return lax.all_to_all(array, axis, 0, 0, axis_index_groups=groups, tiled=True)

    ints = pack_ints(block_count, owner_index, subgrid_index, offsets, station_pair, slot_owner,
                     lax.axis_index("uv"))
    sent = pack(ints, visibility, coordinate)
    arrived = exchange(sent, "tm")
    meta = meta_of(arrived)
    pieces = exchange(chunk_of(screens, lax.axis_index("tm")), "uv", near)
    piece = pick_near(ints, pieces)
    both = jnp.concatenate([piece, lax.ppermute(piece, "uv", shifts[0])], axis=0)
    later = lax.ppermute(both, "uv", shifts[1])
    pieces = exchange(pick_far(ints, (both, later)), "uv", near)
    x = grid_blocks(meta, ints, arrived.reshape(PEERS * PER, 16, LANES))
    meta, x = lax.optimization_barrier((meta, x))
    wanted = exchange(asked(meta, pieces), "tm")
    return screen_product(x, wanted)


def solution(mesh):
    placed = (
        P(None, "uv", "tm", None, None),
        P(None, "uv", "tm", None, None),
        P(None, "uv", "tm"),
        P(None, "uv", "tm", None),
        P(None, "uv", "tm"),
        P("uv", "tm", None),
        P("uv", "tm", None),
        P("uv", None, None, None),
        P(),
    )
    return jax.shard_map(
        on_device, mesh=mesh, in_specs=placed, out_specs=P("uv", "tm", None, None), check_vma=False
    )
```

```python
import jax
import jax.numpy as jnp
from jax import lax
from jax.experimental import pallas as pl
from jax.experimental.pallas import tpu as pltpu
from jax.sharding import PartitionSpec as P

SLOTS = 3
SIDE = 32
BLOCKS = 16
PEERS = 16
CAP = 2
SUBS = 4
STATIONS = 64
PER = SLOTS * CAP
NEAR = 16
FAR = 4
ST_PIECE = STATIONS // NEAR
REQS = 2 * SUBS
LANES = 128
F32 = jnp.float32
BF16 = jnp.bfloat16

ROWS = 64
U_ROW = PER * 8
V_ROW = U_ROW + PER
META_ROW = V_ROW + PER
META = 32
PAIR_LANE = 16

COS_POLY = (1.0, -19.73920440673828, 64.93911743164062, -85.45014190673828, 60.167633056640625,
            -25.967601776123047, 6.528658866882324)
SIN_POLY = (6.283185005187988, -41.341590881347656, 81.59994506835938, -76.6144790649414,
            41.34288787841797, -12.471244812011719)


def smem():
    return pl.BlockSpec(memory_space=pltpu.SMEM)


def vmem():
    return pl.BlockSpec(memory_space=pltpu.VMEM)


def room():
    return pltpu.CompilerParams(vmem_limit_bytes=8 * 1024 * 1024)


def horner(x, poly):
    total = jnp.full_like(x, poly[-1])
    for coefficient in poly[-2::-1]:
        total = total * x + coefficient
    return total


def cis(turns):
    part = turns - jnp.floor(turns + 0.5)
    square = part * part
    return horner(square, COS_POLY), horner(square, SIN_POLY) * part


def times(a, b):
    return a[0] * b[0] - a[1] * b[1], a[0] * b[1] + a[1] * b[0]


def pack_kernel(owners, subs, counts, pair, vis_ref, coord_ref, out_ref, taken, stage):
    lane = lax.broadcasted_iota(jnp.int32, (1, LANES), 1)
    pairs = jnp.zeros((1, LANES), F32)
    for j in range(REQS):
        pairs = jnp.where(lane == PAIR_LANE + j, pair[0, j % 2, j // 2].astype(F32), pairs)
    last = lax.broadcasted_iota(jnp.int32, (8, LANES), 0) == META_ROW % 8
    last = jnp.where(last, pairs, 0.0)

    @pl.loop(0, PEERS)
    def _(o):
        stage[o, 0:ROWS - 16, :] = jnp.zeros((ROWS - 16, LANES), F32)
        for half in (16, 8):
            first = ROWS - half
            stage[o, first:first + 8, :] = last if META_ROW // 8 * 8 == first else jnp.zeros_like(last)

    for slot in range(SLOTS):
        for o in range(PEERS):
            taken[o] = 0

        @pl.loop(0, BLOCKS)
        def _(i):
            owner = owners[slot, 0, i]
            rank = taken[owner]
            taken[owner] = rank + 1
            k = slot * CAP + rank
            values = vis_ref[slot, 0, i].astype(F32)
            values = jnp.where(lane < counts[slot, 0, i], values, 0.0)
            stage[owner, pl.ds(pl.multiple_of(k * 8, 8), 8), :] = values
            where = coord_ref[slot, 0, i].astype(F32)
            stage[owner, pl.ds(U_ROW + k, 1), :] = where[0:1]
            stage[owner, pl.ds(V_ROW + k, 1), :] = where[1:2]
            meta = jnp.where(lane == 2 * k, subs[slot, 0, i].astype(F32), jnp.where(lane == 2 * k + 1, 1.0, 0.0))
            stage[owner, META_ROW:META_ROW + 1, :] += meta

    @pl.loop(0, PEERS)
    def _(o):
        out_ref[o] = stage[o].astype(BF16)


def pack(owners, subs, counts, pair, visibility, coordinate, **kw):
    return pl.pallas_call(
        pack_kernel,
        out_shape=jax.ShapeDtypeStruct((PEERS, ROWS, LANES), BF16),
        in_specs=[smem()] * 4 + [vmem(), vmem()],
        out_specs=vmem(),
        scratch_shapes=[pltpu.SMEM((PEERS,), jnp.int32), pltpu.VMEM((PEERS, ROWS, LANES), F32)],
        name="pack_blocks",
        cost_estimate=pl.CostEstimate(flops=2000000, bytes_accessed=600000, transcendentals=0),
        compiler_params=room(),
        **kw,
    )(owners, subs, counts, pair, visibility, coordinate)


def block_transpose(rows):
    lane = lax.broadcasted_iota(jnp.int32, (8, LANES), 1)
    rows = list(rows)
    for bit in range(2):
        step = SIDE << bit
        upper = (lane & step) != 0
        for low in range(4):
            if low >> bit & 1:
                continue
            high = low | 1 << bit
            x, y = rows[low], rows[high]
            rows[low] = jnp.where(upper, pltpu.roll(y, step, 1), x)
            rows[high] = jnp.where(upper, y, pltpu.roll(x, LANES - step, 1))
    return rows


BATCH = 4


def grid_kernel(meta, offs, rows_ref, x_ref, acc, coords, order, bucket):
    acc[...] = jnp.zeros_like(acc)
    for t in range(PEERS):
        coords[t] = rows_ref[t, ROWS - 16:ROWS, :].astype(F32)

    def gather(t, carry):
        count, spare = carry
        for k in range(PER):
            b = t * PER + k
            sub = meta[t * META + 2 * k]
            live = meta[t * META + 2 * k + 1]
            order[count] = b
            bucket[count] = (k // CAP) * SUBS + sub
            spare = jnp.where(live == 0, b, spare)
            count = count + live
        return count, spare

    count, spare = lax.fori_loop(0, PEERS, gather, (jnp.int32(0), jnp.int32(0)))
    for j in range(BATCH):
        order[count + j] = spare
        bucket[count + j] = 0

    sublane = lax.broadcasted_iota(jnp.int32, (8, LANES), 0).astype(F32)
    seed_l = (sublane * 4.0 - 16.0) * (1.0 / SIDE)
    seed_m = (sublane - 16.0) * (1.0 / SIDE)

    @pl.loop(0, (count + (BATCH - 1)) // BATCH)
    def _(step):
        for j in range(BATCH):
            b = order[step * BATCH + j]
            key = bucket[step * BATCH + j]
            sub = key % SUBS
            t = b // PER
            k = b % PER
            tile = rows_ref[t, pl.ds(pl.multiple_of(k // CAP * 16, 16), 16), :].astype(F32)
            tile = jnp.where(k % CAP == 0, tile[0:8], tile[8:16])
            u = coords[t, pl.ds(U_ROW - (ROWS - 16) + k, 1), :]
            v = coords[t, pl.ds(V_ROW - (ROWS - 16) + k, 1), :]
            du = jnp.broadcast_to(u - offs[0, 0, sub].astype(F32), (8, LANES))
            dv = jnp.broadcast_to(v - offs[0, 1, sub].astype(F32), (8, LANES))
            turn_l = cis(du * (1.0 / SIDE))
            turn_m = cis(dv * (8.0 / SIDE))
            current = cis(du * seed_l)
            cos_rows, sin_rows = [current[0]], [current[1]]
            for _ in range(3):
                current = times(current, turn_l)
                cos_rows.append(current[0])
                sin_rows.append(current[1])
            left = jnp.concatenate(cos_rows + sin_rows, axis=0).astype(BF16)
            phase = [cis(dv * seed_m)]
            for _ in range(3):
                phase.append(times(phase[-1], turn_m))
            real_rows, imag_rows = [], []
            for p in range(4):
                vis = tile[p:p + 1, :], tile[4 + p:5 + p, :]
                for m in range(4):
                    real, imag = times(vis, phase[m])
                    real_rows.append(real)
                    imag_rows.append(imag)
            right = jnp.concatenate(real_rows + imag_rows, axis=0).astype(BF16)
            acc[key] += lax.dot_general(
                left, right, (((1,), (1,)), ((), ())), preferred_element_type=F32
            )

    @pl.loop(0, SLOTS * SUBS)
    def _(key):
        upper = acc[key, 0:SIDE, :]
        lower = acc[key, SIDE:2 * SIDE, :]
        real = upper[:, :LANES] - lower[:, LANES:]
        imag = upper[:, LANES:] + lower[:, :LANES]
        for part, image in enumerate((real, imag)):
            for p, plane in enumerate(block_transpose([image[8 * b:8 * b + 8] for b in range(4)])):
                x_ref[key, 4 * part + p] = plane


def grid_blocks(meta, offs, rows, **kw):
    return pl.pallas_call(
        grid_kernel,
        out_shape=jax.ShapeDtypeStruct((SLOTS * SUBS, 8, 8, LANES), F32),
        in_specs=[smem(), smem(), vmem()],
        out_specs=vmem(),
        scratch_shapes=[
            pltpu.VMEM((SLOTS * SUBS, 2 * SIDE, 8 * SIDE), F32),
            pltpu.VMEM((PEERS, 16, LANES), F32),
            pltpu.SMEM((PEERS * PER + BATCH,), jnp.int32),
            pltpu.SMEM((PEERS * PER + BATCH,), jnp.int32),
        ],
        name="grid_blocks",
        cost_estimate=pl.CostEstimate(flops=800000000, bytes_accessed=800000, transcendentals=0),
        compiler_params=room(),
        **kw,
    )(meta, offs, rows)


def chunk_kernel(t_ref, in_ref, out_ref):
    odd = t_ref[0] % 2 == 1
    low = lax.broadcasted_iota(jnp.int32, (8, LANES), 0) < 4

    def two(first, second):
        a, b = in_ref[0, first].astype(F32), in_ref[0, second].astype(F32)
        a, b = jnp.where(odd, pltpu.roll(a, 4, 0), a), jnp.where(odd, b, pltpu.roll(b, 4, 0))
        return jnp.where(low, a, b)

    for j in range(NEAR):
        first = j * ST_PIECE
        out_ref[j] = jnp.concatenate([two(first, first + 1), two(first + 2, first + 3)], axis=0).astype(BF16)


def chunk_of(screens, t, **kw):
    return pl.pallas_call(
        chunk_kernel,
        out_shape=jax.ShapeDtypeStruct((NEAR, ST_PIECE * 4, LANES), BF16),
        grid_spec=pltpu.PrefetchScalarGridSpec(
            num_scalar_prefetch=1,
            grid=(1,),
            in_specs=[pl.BlockSpec((1, STATIONS, 8, LANES), lambda i, t: (0, 0, 0, t[0] // 2))],
            out_specs=pl.BlockSpec((NEAR, ST_PIECE * 4, LANES), lambda i, t: (0, 0, 0)),
        ),
        name="cut_chunk",
        compiler_params=room(),
        **kw,
    )(t.reshape(1), screens)


def pick_near_kernel(roots, in_ref, out_ref):
    for s in range(SLOTS):
        piece = in_ref[roots[s] % NEAR]
        for k in range(FAR):
            out_ref[k, s] = piece


def pick_near(roots, pieces, **kw):
    return pl.pallas_call(
        pick_near_kernel,
        out_shape=jax.ShapeDtypeStruct((FAR, SLOTS, 16, LANES), BF16),
        in_specs=[smem(), vmem()],
        out_specs=vmem(),
        name="pick_near",
        compiler_params=room(),
        **kw,
    )(roots, pieces)


def pick_far_kernel(roots, in_ref, out_ref):
    pieces = [in_ref[roots[s] // NEAR, s].astype(F32) for s in range(SLOTS)]
    rows = jnp.concatenate(
        [pieces[s][4 * i:4 * i + 4] for i in range(ST_PIECE) for s in range(SLOTS)], axis=0
    ).astype(BF16)
    for j in range(NEAR):
        out_ref[j] = rows


def pick_far(roots, pieces, **kw):
    return pl.pallas_call(
        pick_far_kernel,
        out_shape=jax.ShapeDtypeStruct((NEAR, ST_PIECE * SLOTS * 4, LANES), BF16),
        in_specs=[smem(), vmem()],
        out_specs=vmem(),
        name="pick_far",
        compiler_params=room(),
        **kw,
    )(roots, pieces)


ROWS_ST = SLOTS * 4


def asked_kernel(meta, in_ref, out_ref, table, stage):
    for z in range(NEAR):
        wide = in_ref[z].astype(F32)
        for i in range(ST_PIECE):
            table[z * ST_PIECE + i, 0:ROWS_ST, :] = wide[ROWS_ST * i:ROWS_ST * (i + 1)]

    @pl.loop(0, PEERS)
    def _(t):
        for r in range(REQS):
            station = meta[t * META + PAIR_LANE + r]
            stage[ROWS_ST * r:ROWS_ST * (r + 1), :] = table[station, 0:ROWS_ST, :]
        out_ref[t] = stage[...].astype(BF16)


def asked(meta, pieces, **kw):
    return pl.pallas_call(
        asked_kernel,
        out_shape=jax.ShapeDtypeStruct((PEERS, REQS * ROWS_ST, LANES), BF16),
        in_specs=[smem(), vmem()],
        out_specs=vmem(),
        scratch_shapes=[
            pltpu.VMEM((STATIONS, 16, LANES), F32),
            pltpu.VMEM((REQS * ROWS_ST, LANES), F32),
        ],
        name="asked_stations",
        cost_estimate=pl.CostEstimate(flops=1000000, bytes_accessed=600000, transcendentals=0),
        compiler_params=room(),
        **kw,
    )(meta, pieces)


def screen_kernel(x_ref, in_ref, out_ref, wide, tmp):
    rows = REQS * ROWS_ST
    for t in range(PEERS):
        wide[rows * t:rows * (t + 1), :] = in_ref[t].astype(F32)

    def entry(request, slot, p, half):
        start = half * rows + request * ROWS_ST + slot * 4 + p
        return wide[pl.ds(start, 8, stride=2 * rows), :]

    def product(first, second):
        result = []
        for i in range(2):
            for j in range(2):
                one = times(first[2 * i], second[j])
                two = times(first[2 * i + 1], second[2 + j])
                result.append((one[0] + two[0], one[1] + two[1]))
        return result

    for sub in range(SUBS):
        total = None
        for slot in range(SLOTS):
            first = [(entry(2 * sub, slot, p, 0), entry(2 * sub, slot, p, 1)) for p in range(4)]
            second = [(entry(2 * sub + 1, slot, p, 0), -entry(2 * sub + 1, slot, p, 1)) for p in (0, 2, 1, 3)]
            key = slot * SUBS + sub
            image = [(x_ref[key, p], x_ref[key, 4 + p]) for p in range(4)]
            part = product(product(first, image), second)
            if total is None:
                total = part
            else:
                total = [(a[0] + b[0], a[1] + b[1]) for a, b in zip(total, part)]
        for p in range(4):
            tmp[8 * p:8 * p + 8, :] = total[p][0]
            tmp[32 + 8 * p:40 + 8 * p, :] = total[p][1]
        for a in range(8):
            out_ref[0, sub, :, LANES * a:LANES * (a + 1)] = tmp[pl.ds(a, 8, stride=8), :]


def screen_product(x, screens, **kw):
    return pl.pallas_call(
        screen_kernel,
        out_shape=jax.ShapeDtypeStruct((1, SUBS, 8, SIDE * SIDE), F32),
        in_specs=[vmem(), vmem()],
        out_specs=vmem(),
        scratch_shapes=[
            pltpu.VMEM((PEERS * REQS * ROWS_ST, LANES), F32),
            pltpu.VMEM((64, LANES), F32),
        ],
        name="screen_product",
        cost_estimate=pl.CostEstimate(flops=3000000, bytes_accessed=1000000, transcendentals=0),
        compiler_params=room(),
        **kw,
    )(x, screens)


def meta_of(arrived):
    return arrived[:, META_ROW, :META].astype(jnp.int32).reshape(-1)


def on_device(visibility, coordinate, block_count, owner_index, subgrid_index, offsets,
              station_pair, screens, slot_owner):
    near = [[k * NEAR + j for j in range(NEAR)] for k in range(FAR)]
    far = [[k * NEAR + j for k in range(FAR)] for j in range(NEAR)]

    def exchange(array, axis, groups=None):
        return lax.all_to_all(array, axis, 0, 0, axis_index_groups=groups, tiled=True)

    pieces = exchange(chunk_of(screens, lax.axis_index("tm")), "uv", near)
    pieces = exchange(pick_near(slot_owner, pieces), "uv", far)
    sent = pack(owner_index[..., 0], subgrid_index, block_count, station_pair.swapaxes(1, 2), visibility, coordinate)
    arrived = exchange(sent, "tm")
    meta = meta_of(arrived)
    pieces = exchange(pick_far(slot_owner, pieces), "uv", near)
    x = grid_blocks(meta, offsets.swapaxes(1, 2), arrived)
    meta, x = lax.optimization_barrier((meta, x))
    wanted = exchange(asked(meta, pieces), "tm")
    return screen_product(x, wanted)


def solution(mesh):
    placed = (
        P(None, "uv", "tm", None, None),
        P(None, "uv", "tm", None, None),
        P(None, "uv", "tm"),
        P(None, "uv", "tm", None),
        P(None, "uv", "tm"),
        P("uv", "tm", None),
        P("uv", "tm", None),
        P("uv", None, None, None),
        P(),
    )
    return jax.shard_map(
        on_device, mesh=mesh, in_specs=placed, out_specs=P("uv", "tm", None, None), check_vma=False
    )
```

```python
import jax
import jax.numpy as jnp
from jax import lax
from jax.experimental import pallas as pl
from jax.experimental.pallas import tpu as pltpu
from jax.sharding import PartitionSpec as P

SLOTS = 3
SIDE = 32
BLOCKS = 16
PEERS = 16
CAP = 2
SUBS = 4
STATIONS = 64
PER = SLOTS * CAP
NEAR = 16
FAR = 4
ST_PIECE = STATIONS // NEAR
REQS = 2 * SUBS
LANES = 128
F32 = jnp.float32
BF16 = jnp.bfloat16

ROWS = 64
U_ROW = PER * 8
V_ROW = U_ROW + PER
META_ROW = V_ROW + PER
META = 32
PAIR_LANE = 16

COS_POLY = (1.0, -19.73920440673828, 64.93911743164062, -85.45014190673828, 60.167633056640625,
            -25.967601776123047, 6.528658866882324)
SIN_POLY = (6.283185005187988, -41.341590881347656, 81.59994506835938, -76.6144790649414,
            41.34288787841797, -12.471244812011719)


def smem():
    return pl.BlockSpec(memory_space=pltpu.SMEM)


def vmem():
    return pl.BlockSpec(memory_space=pltpu.VMEM)


def room():
    return pltpu.CompilerParams(vmem_limit_bytes=8 * 1024 * 1024)


def horner(x, poly):
    total = jnp.full_like(x, poly[-1])
    for coefficient in poly[-2::-1]:
        total = total * x + coefficient
    return total


def cis(turns):
    part = turns - jnp.floor(turns + 0.5)
    square = part * part
    return horner(square, COS_POLY), horner(square, SIN_POLY) * part


def times(a, b):
    return a[0] * b[0] - a[1] * b[1], a[0] * b[1] + a[1] * b[0]


def pack_kernel(owners, subs, counts, pair, vis_ref, coord_ref, out_ref, taken, stage):
    lane = lax.broadcasted_iota(jnp.int32, (1, LANES), 1)
    pairs = jnp.zeros((1, LANES), F32)
    for j in range(REQS):
        pairs = jnp.where(lane == PAIR_LANE + j, pair[0, j % 2, j // 2].astype(F32), pairs)
    last = lax.broadcasted_iota(jnp.int32, (8, LANES), 0) == META_ROW % 8
    last = jnp.where(last, pairs, 0.0)

    @pl.loop(0, PEERS)
    def _(o):
        stage[o, 0:ROWS - 16, :] = jnp.zeros((ROWS - 16, LANES), F32)
        for half in (16, 8):
            first = ROWS - half
            stage[o, first:first + 8, :] = last if META_ROW // 8 * 8 == first else jnp.zeros_like(last)

    for slot in range(SLOTS):
        for o in range(PEERS):
            taken[o] = 0

        @pl.loop(0, BLOCKS)
        def _(i):
            owner = owners[slot, 0, i]
            rank = taken[owner]
            taken[owner] = rank + 1
            k = slot * CAP + rank
            values = vis_ref[slot, 0, i].astype(F32)
            values = jnp.where(lane < counts[slot, 0, i], values, 0.0)
            stage[owner, pl.ds(pl.multiple_of(k * 8, 8), 8), :] = values
            where = coord_ref[slot, 0, i].astype(F32)
            stage[owner, pl.ds(U_ROW + k, 1), :] = where[0:1]
            stage[owner, pl.ds(V_ROW + k, 1), :] = where[1:2]
            meta = jnp.where(lane == 2 * k, subs[slot, 0, i].astype(F32), jnp.where(lane == 2 * k + 1, 1.0, 0.0))
            stage[owner, META_ROW:META_ROW + 1, :] += meta

    @pl.loop(0, PEERS)
    def _(o):
        out_ref[o] = stage[o].astype(BF16)


def pack(owners, subs, counts, pair, visibility, coordinate, **kw):
    return pl.pallas_call(
        pack_kernel,
        out_shape=jax.ShapeDtypeStruct((PEERS, ROWS, LANES), BF16),
        in_specs=[smem()] * 4 + [vmem(), vmem()],
        out_specs=vmem(),
        scratch_shapes=[pltpu.SMEM((PEERS,), jnp.int32), pltpu.VMEM((PEERS, ROWS, LANES), F32)],
        name="pack_blocks",
        cost_estimate=pl.CostEstimate(flops=2000000, bytes_accessed=600000, transcendentals=0),
        compiler_params=room(),
        **kw,
    )(owners, subs, counts, pair, visibility, coordinate)


def block_transpose(rows):
    lane = lax.broadcasted_iota(jnp.int32, (8, LANES), 1)
    rows = list(rows)
    for bit in range(2):
        step = SIDE << bit
        upper = (lane & step) != 0
        for low in range(4):
            if low >> bit & 1:
                continue
            high = low | 1 << bit
            x, y = rows[low], rows[high]
            rows[low] = jnp.where(upper, pltpu.roll(y, step, 1), x)
            rows[high] = jnp.where(upper, y, pltpu.roll(x, LANES - step, 1))
    return rows


BATCH = 4


def grid_kernel(meta, offs, rows_ref, x_ref, acc, coords, order, bucket):
    acc[...] = jnp.zeros_like(acc)
    for t in range(PEERS):
        coords[t] = rows_ref[t, ROWS - 16:ROWS, :].astype(F32)

    def gather(t, carry):
        count, spare = carry
        for k in range(PER):
            b = t * PER + k
            sub = meta[t * META + 2 * k]
            live = meta[t * META + 2 * k + 1]
            order[count] = b
            bucket[count] = (k // CAP) * SUBS + sub
            spare = jnp.where(live == 0, b, spare)
            count = count + live
        return count, spare

    count, spare = lax.fori_loop(0, PEERS, gather, (jnp.int32(0), jnp.int32(0)))
    for j in range(BATCH):
        order[count + j] = spare
        bucket[count + j] = 0

    sublane = lax.broadcasted_iota(jnp.int32, (8, LANES), 0).astype(F32)
    seed_l = (sublane * 4.0 - 16.0) * (1.0 / SIDE)
    seed_m = (sublane - 16.0) * (1.0 / SIDE)

    @pl.loop(0, (count + (BATCH - 1)) // BATCH)
    def _(step):
        for j in range(BATCH):
            b = order[step * BATCH + j]
            key = bucket[step * BATCH + j]
            sub = key % SUBS
            t = b // PER
            k = b % PER
            tile = rows_ref[t, pl.ds(pl.multiple_of(k // CAP * 16, 16), 16), :].astype(F32)
            tile = jnp.where(k % CAP == 0, tile[0:8], tile[8:16])
            u = coords[t, pl.ds(U_ROW - (ROWS - 16) + k, 1), :]
            v = coords[t, pl.ds(V_ROW - (ROWS - 16) + k, 1), :]
            du = jnp.broadcast_to(u - offs[0, 0, sub].astype(F32), (8, LANES))
            dv = jnp.broadcast_to(v - offs[0, 1, sub].astype(F32), (8, LANES))
            turn_l = cis(du * (1.0 / SIDE))
            turn_m = cis(dv * (8.0 / SIDE))
            current = cis(du * seed_l)
            cos_rows, sin_rows = [current[0]], [current[1]]
            for _ in range(3):
                current = times(current, turn_l)
                cos_rows.append(current[0])
                sin_rows.append(current[1])
            left = jnp.concatenate(cos_rows + sin_rows, axis=0).astype(BF16)
            phase = [cis(dv * seed_m)]
            for _ in range(3):
                phase.append(times(phase[-1], turn_m))
            real_rows, imag_rows = [], []
            for p in range(4):
                vis = tile[p:p + 1, :], tile[4 + p:5 + p, :]
                for m in range(4):
                    real, imag = times(vis, phase[m])
                    real_rows.append(real)
                    imag_rows.append(imag)
            right = jnp.concatenate(real_rows + imag_rows, axis=0).astype(BF16)
            acc[key] += lax.dot_general(
                left, right, (((1,), (1,)), ((), ())), preferred_element_type=F32
            )

    @pl.loop(0, SLOTS * SUBS)
    def _(key):
        upper = acc[key, 0:SIDE, :]
        lower = acc[key, SIDE:2 * SIDE, :]
        real = upper[:, :LANES] - lower[:, LANES:]
        imag = upper[:, LANES:] + lower[:, :LANES]
        for part, image in enumerate((real, imag)):
            for p, plane in enumerate(block_transpose([image[8 * b:8 * b + 8] for b in range(4)])):
                x_ref[key, 4 * part + p] = plane


def grid_blocks(meta, offs, rows, **kw):
    return pl.pallas_call(
        grid_kernel,
        out_shape=jax.ShapeDtypeStruct((SLOTS * SUBS, 8, 8, LANES), F32),
        in_specs=[smem(), smem(), vmem()],
        out_specs=vmem(),
        scratch_shapes=[
            pltpu.VMEM((SLOTS * SUBS, 2 * SIDE, 8 * SIDE), F32),
            pltpu.VMEM((PEERS, 16, LANES), F32),
            pltpu.SMEM((PEERS * PER + BATCH,), jnp.int32),
            pltpu.SMEM((PEERS * PER + BATCH,), jnp.int32),
        ],
        name="grid_blocks",
        cost_estimate=pl.CostEstimate(flops=800000000, bytes_accessed=800000, transcendentals=0),
        compiler_params=room(),
        **kw,
    )(meta, offs, rows)


def chunk_kernel(t_ref, screens_ref, out_ref, in_ref, arrived):
    lanes = pl.ds(pl.multiple_of(t_ref[0] // 2 * LANES, LANES), LANES)
    copy = pltpu.make_async_copy(screens_ref.at[0, :, :, lanes], in_ref, arrived)
    copy.start()
    copy.wait()
    odd = t_ref[0] % 2 == 1
    low = lax.broadcasted_iota(jnp.int32, (8, LANES), 0) < 4

    def two(first, second):
        a, b = in_ref[first].astype(F32), in_ref[second].astype(F32)
        a, b = jnp.where(odd, pltpu.roll(a, 4, 0), a), jnp.where(odd, b, pltpu.roll(b, 4, 0))
        return jnp.where(low, a, b)

    for j in range(NEAR):
        first = j * ST_PIECE
        out_ref[j] = jnp.concatenate([two(first, first + 1), two(first + 2, first + 3)], axis=0).astype(BF16)


def chunk_of(screens, t, **kw):
    return pl.pallas_call(
        chunk_kernel,
        out_shape=jax.ShapeDtypeStruct((NEAR, ST_PIECE * 4, LANES), BF16),
        in_specs=[smem(), pl.BlockSpec(memory_space=pltpu.HBM)],
        out_specs=vmem(),
        scratch_shapes=[pltpu.VMEM((STATIONS, 8, LANES), BF16), pltpu.SemaphoreType.DMA],
        name="cut_chunk",
        **kw,
    )(t.reshape(1), screens)


def pick_near_kernel(roots, in_ref, out_ref):
    for s in range(SLOTS):
        out_ref[s] = in_ref[roots[s] // FAR]


def pick_near(roots, pieces, **kw):
    return pl.pallas_call(
        pick_near_kernel,
        out_shape=jax.ShapeDtypeStruct((SLOTS, 16, LANES), BF16),
        in_specs=[smem(), vmem()],
        out_specs=vmem(),
        name="pick_near",
        compiler_params=room(),
        **kw,
    )(roots, pieces)


def pick_far_kernel(roots, me, even_ref, odd_ref, out_ref):
    pieces = []
    for s in range(SLOTS):
        shift = (me[0] - roots[s] + FAR * NEAR) % FAR
        k = shift // 2 * SLOTS + s
        pieces.append(jnp.where(shift % 2 == 0, even_ref[k].astype(F32), odd_ref[k].astype(F32)))
    rows = jnp.concatenate(
        [pieces[s][4 * i:4 * i + 4] for i in range(ST_PIECE) for s in range(SLOTS)], axis=0
    ).astype(BF16)
    for j in range(NEAR):
        out_ref[j] = rows


def pick_far(roots, me, even, odd, **kw):
    return pl.pallas_call(
        pick_far_kernel,
        out_shape=jax.ShapeDtypeStruct((NEAR, ST_PIECE * SLOTS * 4, LANES), BF16),
        in_specs=[smem(), smem(), vmem(), vmem()],
        out_specs=vmem(),
        name="pick_far",
        compiler_params=room(),
        **kw,
    )(roots, me.reshape(1), even, odd)


ROWS_ST = SLOTS * 4


def asked_kernel(meta, in_ref, out_ref, table, stage):
    for z in range(NEAR):
        wide = in_ref[z].astype(F32)
        for i in range(ST_PIECE):
            table[z * ST_PIECE + i, 0:ROWS_ST, :] = wide[ROWS_ST * i:ROWS_ST * (i + 1)]

    @pl.loop(0, PEERS)
    def _(t):
        for r in range(REQS):
            station = meta[t * META + PAIR_LANE + r]
            stage[ROWS_ST * r:ROWS_ST * (r + 1), :] = table[station, 0:ROWS_ST, :]
        out_ref[t] = stage[...].astype(BF16)


def asked(meta, pieces, **kw):
    return pl.pallas_call(
        asked_kernel,
        out_shape=jax.ShapeDtypeStruct((PEERS, REQS * ROWS_ST, LANES), BF16),
        in_specs=[smem(), vmem()],
        out_specs=vmem(),
        scratch_shapes=[
            pltpu.VMEM((STATIONS, 16, LANES), F32),
            pltpu.VMEM((REQS * ROWS_ST, LANES), F32),
        ],
        name="asked_stations",
        cost_estimate=pl.CostEstimate(flops=1000000, bytes_accessed=600000, transcendentals=0),
        compiler_params=room(),
        **kw,
    )(meta, pieces)


def screen_kernel(x_ref, in_ref, out_ref, wide, tmp):
    rows = REQS * ROWS_ST
    for t in range(PEERS):
        wide[rows * t:rows * (t + 1), :] = in_ref[t].astype(F32)

    def entry(request, slot, p, half):
        start = half * rows + request * ROWS_ST + slot * 4 + p
        return wide[pl.ds(start, 8, stride=2 * rows), :]

    def product(first, second):
        result = []
        for i in range(2):
            for j in range(2):
                one = times(first[2 * i], second[j])
                two = times(first[2 * i + 1], second[2 + j])
                result.append((one[0] + two[0], one[1] + two[1]))
        return result

    for sub in range(SUBS):
        total = None
        for slot in range(SLOTS):
            first = [(entry(2 * sub, slot, p, 0), entry(2 * sub, slot, p, 1)) for p in range(4)]
            second = [(entry(2 * sub + 1, slot, p, 0), -entry(2 * sub + 1, slot, p, 1)) for p in (0, 2, 1, 3)]
            key = slot * SUBS + sub
            image = [(x_ref[key, p], x_ref[key, 4 + p]) for p in range(4)]
            part = product(product(first, image), second)
            if total is None:
                total = part
            else:
                total = [(a[0] + b[0], a[1] + b[1]) for a, b in zip(total, part)]
        for p in range(4):
            tmp[8 * p:8 * p + 8, :] = total[p][0]
            tmp[32 + 8 * p:40 + 8 * p, :] = total[p][1]
        for a in range(8):
            out_ref[0, sub, :, LANES * a:LANES * (a + 1)] = tmp[pl.ds(a, 8, stride=8), :]


def screen_product(x, screens, **kw):
    return pl.pallas_call(
        screen_kernel,
        out_shape=jax.ShapeDtypeStruct((1, SUBS, 8, SIDE * SIDE), F32),
        in_specs=[vmem(), vmem()],
        out_specs=vmem(),
        scratch_shapes=[
            pltpu.VMEM((PEERS * REQS * ROWS_ST, LANES), F32),
            pltpu.VMEM((64, LANES), F32),
        ],
        name="screen_product",
        cost_estimate=pl.CostEstimate(flops=3000000, bytes_accessed=1000000, transcendentals=0),
        compiler_params=room(),
        **kw,
    )(x, screens)


def meta_of(arrived):
    return arrived[:, META_ROW, :META].astype(jnp.int32).reshape(-1)


def on_device(visibility, coordinate, block_count, owner_index, subgrid_index, offsets,
              station_pair, screens, slot_owner):
    near = [[k * FAR + j for k in range(NEAR)] for j in range(FAR)]

    def shifted(array, shift):
        pairs = [(k * FAR + j, k * FAR + (j + shift) % FAR) for k in range(NEAR) for j in range(FAR)]
        return lax.ppermute(array, "uv", pairs)

    def exchange(array, axis, groups=None):
        return lax.all_to_all(array, axis, 0, 0, axis_index_groups=groups, tiled=True)

    pieces = exchange(chunk_of(screens, lax.axis_index("tm")), "uv", near)
    piece = pick_near(slot_owner, pieces)
    even = jnp.concatenate([piece, shifted(piece, 2)], axis=0)
    odd = shifted(even, 1)
    sent = pack(owner_index[..., 0], subgrid_index, block_count, station_pair.swapaxes(1, 2), visibility, coordinate)
    arrived = exchange(sent, "tm")
    meta = meta_of(arrived)
    pieces = exchange(pick_far(slot_owner, lax.axis_index("uv"), even, odd), "uv", near)
    x = grid_blocks(meta, offsets.swapaxes(1, 2), arrived)
    meta, x = lax.optimization_barrier((meta, x))
    wanted = exchange(asked(meta, pieces), "tm")
    return screen_product(x, wanted)


def solution(mesh):
    placed = (
        P(None, "uv", "tm", None, None),
        P(None, "uv", "tm", None, None),
        P(None, "uv", "tm"),
        P(None, "uv", "tm", None),
        P(None, "uv", "tm"),
        P("uv", "tm", None),
        P("uv", "tm", None),
        P("uv", None, None, None),
        P(),
    )
    return jax.shard_map(
        on_device, mesh=mesh, in_specs=placed, out_specs=P("uv", "tm", None, None), check_vma=False
    )
```

```python
import jax
import jax.numpy as jnp
from jax import lax
from jax.experimental import pallas as pl
from jax.experimental.pallas import tpu as pltpu
from jax.sharding import PartitionSpec as P

SLOTS = 3
SIDE = 32
BLOCKS = 16
PEERS = 16
CAP = 2
SUBS = 4
STATIONS = 64
PER = SLOTS * CAP
NEAR = 16
FAR = 4
ST_PIECE = STATIONS // NEAR
REQS = 2 * SUBS
LANES = 128
F32 = jnp.float32
BF16 = jnp.bfloat16

TOTAL = SLOTS * BLOCKS
U_ROW = TOTAL * 8
V_ROW = U_ROW + TOTAL
META_ROW = V_ROW + TOTAL
ROWS = META_ROW + 16
META = 64

COS_POLY = (1.0, -19.73920440673828, 64.93911743164062, -85.45014190673828, 60.167633056640625,
            -25.967601776123047, 6.528658866882324)
SIN_POLY = (6.283185005187988, -41.341590881347656, 81.59994506835938, -76.6144790649414,
            41.34288787841797, -12.471244812011719)


def smem():
    return pl.BlockSpec(memory_space=pltpu.SMEM)


def vmem():
    return pl.BlockSpec(memory_space=pltpu.VMEM)


def room():
    return pltpu.CompilerParams(vmem_limit_bytes=8 * 1024 * 1024)


def horner(x, poly):
    total = jnp.full_like(x, poly[-1])
    for coefficient in poly[-2::-1]:
        total = total * x + coefficient
    return total


def cis(turns):
    part = turns - jnp.floor(turns + 0.5)
    square = part * part
    return horner(square, COS_POLY), horner(square, SIN_POLY) * part


def times(a, b):
    return a[0] * b[0] - a[1] * b[1], a[0] * b[1] + a[1] * b[0]


def pack_kernel(owners, subs, counts, pair, vis_ref, coord_ref, out_ref, stage):
    lane = lax.broadcasted_iota(jnp.int32, (1, LANES), 1)
    pairs = jnp.zeros((1, LANES), F32)
    for j in range(REQS):
        pairs = jnp.where(lane == j, pair[0, j % 2, j // 2].astype(F32), pairs)
    stage[META_ROW - U_ROW:, :] = jnp.zeros((16, LANES), F32)
    owner_row, sub_row = jnp.zeros((1, LANES), F32), jnp.zeros((1, LANES), F32)
    for slot in range(SLOTS):
        for i in range(0, BLOCKS, 2):
            two = []
            for k in (i, i + 1):
                spot = slot * BLOCKS + k
                values = vis_ref[slot, 0, k].astype(F32)
                two.append(jnp.where(lane < counts[slot, 0, k], values, 0.0))
                where = coord_ref[slot, 0, k].astype(F32)
                stage[spot:spot + 1, :] = where[0:1]
                stage[TOTAL + spot:TOTAL + spot + 1, :] = where[1:2]
                owner_row = jnp.where(lane == spot, owners[slot, 0, k].astype(F32), owner_row)
                sub_row = jnp.where(lane == spot, subs[slot, 0, k].astype(F32), sub_row)
            first = (slot * BLOCKS + i) * 8
            out_ref[first:first + 16, :] = jnp.concatenate(two, axis=0).astype(BF16)
    first = META_ROW - U_ROW
    stage[first:first + 1, :] = owner_row
    stage[first + 1:first + 2, :] = sub_row
    stage[first + 2:first + 3, :] = pairs
    out_ref[U_ROW:, :] = stage[...].astype(BF16)


def pack(owners, subs, counts, pair, visibility, coordinate, **kw):
    return pl.pallas_call(
        pack_kernel,
        out_shape=jax.ShapeDtypeStruct((ROWS, LANES), BF16),
        in_specs=[smem()] * 4 + [vmem(), vmem()],
        out_specs=vmem(),
        scratch_shapes=[pltpu.VMEM((ROWS - U_ROW, LANES), F32)],
        name="pack_blocks",
        cost_estimate=pl.CostEstimate(flops=2000000, bytes_accessed=600000, transcendentals=0),
        compiler_params=room(),
        **kw,
    )(owners, subs, counts, pair, visibility, coordinate)


def block_transpose(rows):
    lane = lax.broadcasted_iota(jnp.int32, (8, LANES), 1)
    rows = list(rows)
    for bit in range(2):
        step = SIDE << bit
        upper = (lane & step) != 0
        for low in range(4):
            if low >> bit & 1:
                continue
            high = low | 1 << bit
            x, y = rows[low], rows[high]
            rows[low] = jnp.where(upper, pltpu.roll(y, step, 1), x)
            rows[high] = jnp.where(upper, y, pltpu.roll(x, LANES - step, 1))
    return rows


BATCH = 4


def grid_kernel(me, meta, offs, rows_ref, x_ref, acc, coords, order, bucket):
    acc[...] = jnp.zeros_like(acc)
    for t in range(PEERS):
        coords[t] = rows_ref[t, U_ROW:META_ROW, :].astype(F32)
    for j in range(PEERS * PER + BATCH):
        order[j] = 0
        bucket[j] = 0

    def gather(t, count):
        for i in range(TOTAL):
            first = t * (3 * META) + i
            order[count] = t * TOTAL + i
            bucket[count] = (i // BLOCKS) * SUBS + meta[first + META]
            count = count + (meta[first] == me[0]).astype(jnp.int32)
        return count

    count = lax.fori_loop(0, PEERS, gather, jnp.int32(0))

    sublane = lax.broadcasted_iota(jnp.int32, (8, LANES), 0).astype(F32)
    seed_l = (sublane * 4.0 - 16.0) * (1.0 / SIDE)
    seed_m = (sublane - 16.0) * (1.0 / SIDE)

    @pl.loop(0, (count + (BATCH - 1)) // BATCH)
    def _(step):
        for j in range(BATCH):
            b = order[step * BATCH + j]
            key = bucket[step * BATCH + j]
            sub = key % SUBS
            t = b // TOTAL
            k = b % TOTAL
            tile = rows_ref[t, pl.ds(pl.multiple_of(k // 2 * 16, 16), 16), :].astype(F32)
            tile = jnp.where(k % 2 == 0, tile[0:8], tile[8:16])
            tile = jnp.where(step * BATCH + j < count, tile, 0.0)
            u = coords[t, pl.ds(k, 1), :]
            v = coords[t, pl.ds(TOTAL + k, 1), :]
            du = jnp.broadcast_to(u - offs[0, 0, sub].astype(F32), (8, LANES))
            dv = jnp.broadcast_to(v - offs[0, 1, sub].astype(F32), (8, LANES))
            turn_l = cis(du * (1.0 / SIDE))
            turn_m = cis(dv * (8.0 / SIDE))
            current = cis(du * seed_l)
            cos_rows, sin_rows = [current[0]], [current[1]]
            for _ in range(3):
                current = times(current, turn_l)
                cos_rows.append(current[0])
                sin_rows.append(current[1])
            left = jnp.concatenate(cos_rows + sin_rows, axis=0).astype(BF16)
            phase = [cis(dv * seed_m)]
            for _ in range(3):
                phase.append(times(phase[-1], turn_m))
            real_rows, imag_rows = [], []
            for p in range(4):
                vis = tile[p:p + 1, :], tile[4 + p:5 + p, :]
                for m in range(4):
                    real, imag = times(vis, phase[m])
                    real_rows.append(real)
                    imag_rows.append(imag)
            right = jnp.concatenate(real_rows + imag_rows, axis=0).astype(BF16)
            acc[key] += lax.dot_general(
                left, right, (((1,), (1,)), ((), ())), preferred_element_type=F32
            )

    @pl.loop(0, SLOTS * SUBS)
    def _(key):
        upper = acc[key, 0:SIDE, :]
        lower = acc[key, SIDE:2 * SIDE, :]
        real = upper[:, :LANES] - lower[:, LANES:]
        imag = upper[:, LANES:] + lower[:, :LANES]
        for part, image in enumerate((real, imag)):
            for p, plane in enumerate(block_transpose([image[8 * b:8 * b + 8] for b in range(4)])):
                x_ref[key, 4 * part + p] = plane


def grid_blocks(me, meta, offs, rows, **kw):
    return pl.pallas_call(
        grid_kernel,
        out_shape=jax.ShapeDtypeStruct((SLOTS * SUBS, 8, 8, LANES), F32),
        in_specs=[smem(), smem(), smem(), vmem()],
        out_specs=vmem(),
        scratch_shapes=[
            pltpu.VMEM((SLOTS * SUBS, 2 * SIDE, 8 * SIDE), F32),
            pltpu.VMEM((PEERS, 2 * TOTAL, LANES), F32),
            pltpu.SMEM((PEERS * PER + BATCH,), jnp.int32),
            pltpu.SMEM((PEERS * PER + BATCH,), jnp.int32),
        ],
        name="grid_blocks",
        cost_estimate=pl.CostEstimate(flops=800000000, bytes_accessed=800000, transcendentals=0),
        compiler_params=room(),
        **kw,
    )(me.reshape(1), meta, offs, rows)


COPIES = 4


def chunk_kernel(t_ref, screens_ref, out_ref, in_ref, arrived):
    lanes = pl.ds(pl.multiple_of(t_ref[0] // 2 * LANES, LANES), LANES)
    share = STATIONS // COPIES
    copies = []
    for c in range(COPIES):
        some = pl.ds(c * share, share)
        copies.append(pltpu.make_async_copy(screens_ref.at[0, some, :, lanes], in_ref.at[some], arrived.at[c]))
        copies[-1].start()
    odd = t_ref[0] % 2 == 1
    low = lax.broadcasted_iota(jnp.int32, (8, LANES), 0) < 4

    def two(first, second):
        a, b = in_ref[first].astype(F32), in_ref[second].astype(F32)
        a, b = jnp.where(odd, pltpu.roll(a, 4, 0), a), jnp.where(odd, b, pltpu.roll(b, 4, 0))
        return jnp.where(low, a, b)

    for j in range(NEAR):
        first = j * ST_PIECE
        if first % share == 0:
            copies[first // share].wait()
        out_ref[j] = jnp.concatenate([two(first, first + 1), two(first + 2, first + 3)], axis=0).astype(BF16)


def chunk_of(screens, t, **kw):
    return pl.pallas_call(
        chunk_kernel,
        out_shape=jax.ShapeDtypeStruct((NEAR, ST_PIECE * 4, LANES), BF16),
        in_specs=[smem(), pl.BlockSpec(memory_space=pltpu.HBM)],
        out_specs=vmem(),
        scratch_shapes=[pltpu.VMEM((STATIONS, 8, LANES), BF16), pltpu.SemaphoreType.DMA((COPIES,))],
        name="cut_chunk",
        **kw,
    )(t.reshape(1), screens)


def pick_near_kernel(roots, in_ref, out_ref):
    for s in range(SLOTS):
        out_ref[s] = in_ref[roots[s] // FAR]


def pick_near(roots, pieces, **kw):
    return pl.pallas_call(
        pick_near_kernel,
        out_shape=jax.ShapeDtypeStruct((SLOTS, 16, LANES), BF16),
        in_specs=[smem(), vmem()],
        out_specs=vmem(),
        name="pick_near",
        compiler_params=room(),
        **kw,
    )(roots, pieces)


def pick_far_kernel(roots, me, even_ref, odd_ref, out_ref):
    pieces = []
    for s in range(SLOTS):
        shift = (me[0] - roots[s] + FAR * NEAR) % FAR
        k = shift // 2 * SLOTS + s
        pieces.append(jnp.where(shift % 2 == 0, even_ref[k].astype(F32), odd_ref[k].astype(F32)))
    rows = jnp.concatenate(
        [pieces[s][4 * i:4 * i + 4] for i in range(ST_PIECE) for s in range(SLOTS)], axis=0
    ).astype(BF16)
    for j in range(NEAR):
        out_ref[j] = rows


def pick_far(roots, me, even, odd, **kw):
    return pl.pallas_call(
        pick_far_kernel,
        out_shape=jax.ShapeDtypeStruct((NEAR, ST_PIECE * SLOTS * 4, LANES), BF16),
        in_specs=[smem(), smem(), vmem(), vmem()],
        out_specs=vmem(),
        name="pick_far",
        compiler_params=room(),
        **kw,
    )(roots, me.reshape(1), even, odd)


ROWS_ST = SLOTS * 4


def asked_kernel(meta, in_ref, out_ref, table, stage):
    for z in range(NEAR):
        wide = in_ref[z].astype(F32)
        for i in range(ST_PIECE):
            table[z * ST_PIECE + i, 0:ROWS_ST, :] = wide[ROWS_ST * i:ROWS_ST * (i + 1)]

    @pl.loop(0, PEERS)
    def _(t):
        for r in range(REQS):
            station = meta[t * (3 * META) + 2 * META + r]
            stage[ROWS_ST * r:ROWS_ST * (r + 1), :] = table[station, 0:ROWS_ST, :]
        out_ref[t] = stage[...].astype(BF16)


def asked(meta, pieces, **kw):
    return pl.pallas_call(
        asked_kernel,
        out_shape=jax.ShapeDtypeStruct((PEERS, REQS * ROWS_ST, LANES), BF16),
        in_specs=[smem(), vmem()],
        out_specs=vmem(),
        scratch_shapes=[
            pltpu.VMEM((STATIONS, 16, LANES), F32),
            pltpu.VMEM((REQS * ROWS_ST, LANES), F32),
        ],
        name="asked_stations",
        cost_estimate=pl.CostEstimate(flops=1000000, bytes_accessed=600000, transcendentals=0),
        compiler_params=room(),
        **kw,
    )(meta, pieces)


def screen_kernel(x_ref, in_ref, out_ref, wide, tmp):
    rows = REQS * ROWS_ST
    for t in range(PEERS):
        wide[rows * t:rows * (t + 1), :] = in_ref[t].astype(F32)

    def entry(request, slot, p, half):
        start = half * rows + request * ROWS_ST + slot * 4 + p
        return wide[pl.ds(start, 8, stride=2 * rows), :]

    def product(first, second):
        result = []
        for i in range(2):
            for j in range(2):
                one = times(first[2 * i], second[j])
                two = times(first[2 * i + 1], second[2 + j])
                result.append((one[0] + two[0], one[1] + two[1]))
        return result

    for sub in range(SUBS):
        total = None
        for slot in range(SLOTS):
            first = [(entry(2 * sub, slot, p, 0), entry(2 * sub, slot, p, 1)) for p in range(4)]
            second = [(entry(2 * sub + 1, slot, p, 0), -entry(2 * sub + 1, slot, p, 1)) for p in (0, 2, 1, 3)]
            key = slot * SUBS + sub
            image = [(x_ref[key, p], x_ref[key, 4 + p]) for p in range(4)]
            part = product(product(first, image), second)
            if total is None:
                total = part
            else:
                total = [(a[0] + b[0], a[1] + b[1]) for a, b in zip(total, part)]
        for p in range(4):
            tmp[8 * p:8 * p + 8, :] = total[p][0]
            tmp[32 + 8 * p:40 + 8 * p, :] = total[p][1]
        for a in range(8):
            out_ref[0, sub, :, LANES * a:LANES * (a + 1)] = tmp[pl.ds(a, 8, stride=8), :]


def screen_product(x, screens, **kw):
    return pl.pallas_call(
        screen_kernel,
        out_shape=jax.ShapeDtypeStruct((1, SUBS, 8, SIDE * SIDE), F32),
        in_specs=[vmem(), vmem()],
        out_specs=vmem(),
        scratch_shapes=[
            pltpu.VMEM((PEERS * REQS * ROWS_ST, LANES), F32),
            pltpu.VMEM((64, LANES), F32),
        ],
        name="screen_product",
        cost_estimate=pl.CostEstimate(flops=3000000, bytes_accessed=1000000, transcendentals=0),
        compiler_params=room(),
        **kw,
    )(x, screens)


def meta_of(arrived):
    return arrived[:, META_ROW:META_ROW + 3, :META].astype(jnp.int32).reshape(-1)


def on_device(visibility, coordinate, block_count, owner_index, subgrid_index, offsets,
              station_pair, screens, slot_owner):
    near = [[k * FAR + j for k in range(NEAR)] for j in range(FAR)]

    def shifted(array, shift):
        pairs = [(k * FAR + j, k * FAR + (j + shift) % FAR) for k in range(NEAR) for j in range(FAR)]
        return lax.ppermute(array, "uv", pairs)

    def exchange(array, axis, groups=None):
        return lax.all_to_all(array, axis, 0, 0, axis_index_groups=groups, tiled=True)

    pieces = exchange(chunk_of(screens, lax.axis_index("tm")), "uv", near)
    sent = pack(owner_index[..., 0], subgrid_index, block_count, station_pair.swapaxes(1, 2), visibility, coordinate)
    piece = pick_near(slot_owner, pieces)
    even = jnp.concatenate([piece, shifted(piece, 2)], axis=0)
    odd = shifted(even, 1)
    arrived = lax.all_gather(sent, "tm")
    meta = meta_of(arrived)
    pieces = exchange(pick_far(slot_owner, lax.axis_index("uv"), even, odd), "uv", near)
    x = grid_blocks(lax.axis_index("tm"), meta, offsets.swapaxes(1, 2), arrived)
    meta, x = lax.optimization_barrier((meta, x))
    wanted = exchange(asked(meta, pieces), "tm")
    return screen_product(x, wanted)


def solution(mesh):
    placed = (
        P(None, "uv", "tm", None, None),
        P(None, "uv", "tm", None, None),
        P(None, "uv", "tm"),
        P(None, "uv", "tm", None),
        P(None, "uv", "tm"),
        P("uv", "tm", None),
        P("uv", "tm", None),
        P("uv", None, None, None),
        P(),
    )
    return jax.shard_map(
        on_device, mesh=mesh, in_specs=placed, out_specs=P("uv", "tm", None, None), check_vma=False
    )
```

```python
import jax
import jax.numpy as jnp
from jax import lax
from jax.experimental import pallas as pl
from jax.experimental.pallas import tpu as pltpu
from jax.sharding import PartitionSpec as P

SLOTS = 3
SIDE = 32
BLOCKS = 16
PEERS = 16
CAP = 2
SUBS = 4
STATIONS = 64
PER = SLOTS * CAP
NEAR = 16
FAR = 4
ST_PIECE = STATIONS // NEAR
REQS = 2 * SUBS
LANES = 128
F32 = jnp.float32
BF16 = jnp.bfloat16

ROWS = 64
U_ROW = PER * 8
V_ROW = U_ROW + PER
META_ROW = V_ROW + PER
META = 32
PAIR_LANE = 16

COS_POLY = (1.0, -19.73920440673828, 64.93911743164062, -85.45014190673828, 60.167633056640625,
            -25.967601776123047, 6.528658866882324)
SIN_POLY = (6.283185005187988, -41.341590881347656, 81.59994506835938, -76.6144790649414,
            41.34288787841797, -12.471244812011719)


def smem():
    return pl.BlockSpec(memory_space=pltpu.SMEM)


def vmem():
    return pl.BlockSpec(memory_space=pltpu.VMEM)


def room():
    return pltpu.CompilerParams(vmem_limit_bytes=8 * 1024 * 1024)


def horner(x, poly):
    total = jnp.full_like(x, poly[-1])
    for coefficient in poly[-2::-1]:
        total = total * x + coefficient
    return total


def cis(turns):
    part = turns - jnp.floor(turns + 0.5)
    square = part * part
    return horner(square, COS_POLY), horner(square, SIN_POLY) * part


def times(a, b):
    return a[0] * b[0] - a[1] * b[1], a[0] * b[1] + a[1] * b[0]


def pack_kernel(owners, subs, counts, pair, vis_ref, coord_ref, out_ref, taken, stage):
    lane = lax.broadcasted_iota(jnp.int32, (1, LANES), 1)
    pairs = jnp.zeros((1, LANES), F32)
    for j in range(REQS):
        pairs = jnp.where(lane == PAIR_LANE + j, pair[0, j % 2, j // 2].astype(F32), pairs)
    last = lax.broadcasted_iota(jnp.int32, (8, LANES), 0) == META_ROW % 8
    last = jnp.where(last, pairs, 0.0)

    @pl.loop(0, PEERS)
    def _(o):
        stage[o, 0:ROWS - 16, :] = jnp.zeros((ROWS - 16, LANES), F32)
        for half in (16, 8):
            first = ROWS - half
            stage[o, first:first + 8, :] = last if META_ROW // 8 * 8 == first else jnp.zeros_like(last)

    for slot in range(SLOTS):
        for o in range(PEERS):
            taken[o] = 0

        @pl.loop(0, BLOCKS)
        def _(i):
            owner = owners[slot, 0, i]
            rank = taken[owner]
            taken[owner] = rank + 1
            k = slot * CAP + rank
            values = vis_ref[slot, 0, i].astype(F32)
            values = jnp.where(lane < counts[slot, 0, i], values, 0.0)
            stage[owner, pl.ds(pl.multiple_of(k * 8, 8), 8), :] = values
            where = coord_ref[slot, 0, i].astype(F32)
            stage[owner, pl.ds(U_ROW + k, 1), :] = where[0:1]
            stage[owner, pl.ds(V_ROW + k, 1), :] = where[1:2]
            meta = jnp.where(lane == 2 * k, subs[slot, 0, i].astype(F32), jnp.where(lane == 2 * k + 1, 1.0, 0.0))
            stage[owner, META_ROW:META_ROW + 1, :] += meta

    @pl.loop(0, PEERS)
    def _(o):
        out_ref[o] = stage[o].astype(BF16)


def pack(owners, subs, counts, pair, visibility, coordinate, **kw):
    return pl.pallas_call(
        pack_kernel,
        out_shape=jax.ShapeDtypeStruct((PEERS, ROWS, LANES), BF16),
        in_specs=[smem()] * 4 + [vmem(), vmem()],
        out_specs=vmem(),
        scratch_shapes=[pltpu.SMEM((PEERS,), jnp.int32), pltpu.VMEM((PEERS, ROWS, LANES), F32)],
        name="pack_blocks",
        cost_estimate=pl.CostEstimate(flops=2000000, bytes_accessed=600000, transcendentals=0),
        compiler_params=room(),
        **kw,
    )(owners, subs, counts, pair, visibility, coordinate)


def block_transpose(rows):
    lane = lax.broadcasted_iota(jnp.int32, (8, LANES), 1)
    rows = list(rows)
    for bit in range(2):
        step = SIDE << bit
        upper = (lane & step) != 0
        for low in range(4):
            if low >> bit & 1:
                continue
            high = low | 1 << bit
            x, y = rows[low], rows[high]
            rows[low] = jnp.where(upper, pltpu.roll(y, step, 1), x)
            rows[high] = jnp.where(upper, y, pltpu.roll(x, LANES - step, 1))
    return rows


BATCH = 4


def grid_kernel(meta, offs, rows_ref, x_ref, acc, coords, order, bucket):
    acc[...] = jnp.zeros_like(acc)
    for t in range(PEERS):
        coords[t] = rows_ref[t, ROWS - 16:ROWS, :].astype(F32)

    def gather(t, carry):
        count, spare = carry
        for k in range(PER):
            b = t * PER + k
            sub = meta[t * META + 2 * k]
            live = meta[t * META + 2 * k + 1]
            order[count] = b
            bucket[count] = (k // CAP) * SUBS + sub
            spare = jnp.where(live == 0, b, spare)
            count = count + live
        return count, spare

    count, spare = lax.fori_loop(0, PEERS, gather, (jnp.int32(0), jnp.int32(0)))
    for j in range(BATCH):
        order[count + j] = spare
        bucket[count + j] = 0

    sublane = lax.broadcasted_iota(jnp.int32, (8, LANES), 0).astype(F32)
    seed_l = (sublane * 4.0 - 16.0) * (1.0 / SIDE)
    seed_m = (sublane - 16.0) * (1.0 / SIDE)

    @pl.loop(0, (count + (BATCH - 1)) // BATCH)
    def _(step):
        for j in range(BATCH):
            b = order[step * BATCH + j]
            key = bucket[step * BATCH + j]
            sub = key % SUBS
            t = b // PER
            k = b % PER
            tile = rows_ref[t, pl.ds(pl.multiple_of(k // CAP * 16, 16), 16), :].astype(F32)
            tile = jnp.where(k % CAP == 0, tile[0:8], tile[8:16])
            u = coords[t, pl.ds(U_ROW - (ROWS - 16) + k, 1), :]
            v = coords[t, pl.ds(V_ROW - (ROWS - 16) + k, 1), :]
            du = jnp.broadcast_to(u - offs[0, 0, sub].astype(F32), (8, LANES))
            dv = jnp.broadcast_to(v - offs[0, 1, sub].astype(F32), (8, LANES))
            turn_l = cis(du * (1.0 / SIDE))
            turn_m = cis(dv * (8.0 / SIDE))
            current = cis(du * seed_l)
            cos_rows, sin_rows = [current[0]], [current[1]]
            for _ in range(3):
                current = times(current, turn_l)
                cos_rows.append(current[0])
                sin_rows.append(current[1])
            left = jnp.concatenate(cos_rows + sin_rows, axis=0).astype(BF16)
            phase = [cis(dv * seed_m)]
            for _ in range(3):
                phase.append(times(phase[-1], turn_m))
            real_rows, imag_rows = [], []
            for p in range(4):
                vis = tile[p:p + 1, :], tile[4 + p:5 + p, :]
                for m in range(4):
                    real, imag = times(vis, phase[m])
                    real_rows.append(real)
                    imag_rows.append(imag)
            right = jnp.concatenate(real_rows + imag_rows, axis=0).astype(BF16)
            acc[key] += lax.dot_general(
                left, right, (((1,), (1,)), ((), ())), preferred_element_type=F32
            )

    @pl.loop(0, SLOTS * SUBS)
    def _(key):
        upper = acc[key, 0:SIDE, :]
        lower = acc[key, SIDE:2 * SIDE, :]
        real = upper[:, :LANES] - lower[:, LANES:]
        imag = upper[:, LANES:] + lower[:, :LANES]
        for part, image in enumerate((real, imag)):
            for p, plane in enumerate(block_transpose([image[8 * b:8 * b + 8] for b in range(4)])):
                x_ref[key, 4 * part + p] = plane


def grid_blocks(meta, offs, rows, **kw):
    return pl.pallas_call(
        grid_kernel,
        out_shape=jax.ShapeDtypeStruct((SLOTS * SUBS, 8, 8, LANES), F32),
        in_specs=[smem(), smem(), vmem()],
        out_specs=vmem(),
        scratch_shapes=[
            pltpu.VMEM((SLOTS * SUBS, 2 * SIDE, 8 * SIDE), F32),
            pltpu.VMEM((PEERS, 16, LANES), F32),
            pltpu.SMEM((PEERS * PER + BATCH,), jnp.int32),
            pltpu.SMEM((PEERS * PER + BATCH,), jnp.int32),
        ],
        name="grid_blocks",
        cost_estimate=pl.CostEstimate(flops=800000000, bytes_accessed=800000, transcendentals=0),
        compiler_params=room(),
        **kw,
    )(meta, offs, rows)


COPIES = 4


def chunk_kernel(screens_ref, out_ref, in_ref, arrived):
    t = lax.axis_index("tm")
    lanes = pl.ds(pl.multiple_of(t // 2 * LANES, LANES), LANES)
    share = STATIONS // COPIES
    copies = []
    for c in range(COPIES):
        some = pl.ds(c * share, share)
        copies.append(pltpu.make_async_copy(screens_ref.at[0, some, :, lanes], in_ref.at[some], arrived.at[c]))
        copies[-1].start()
    odd = t % 2 == 1
    low = lax.broadcasted_iota(jnp.int32, (8, LANES), 0) < 4

    def two(first, second):
        a, b = in_ref[first].astype(F32), in_ref[second].astype(F32)
        a, b = jnp.where(odd, pltpu.roll(a, 4, 0), a), jnp.where(odd, b, pltpu.roll(b, 4, 0))
        return jnp.where(low, a, b)

    for j in range(NEAR):
        first = j * ST_PIECE
        if first % share == 0:
            copies[first // share].wait()
        out_ref[j] = jnp.concatenate([two(first, first + 1), two(first + 2, first + 3)], axis=0).astype(BF16)


def chunk_of(screens, **kw):
    return pl.pallas_call(
        chunk_kernel,
        out_shape=jax.ShapeDtypeStruct((NEAR, ST_PIECE * 4, LANES), BF16),
        in_specs=[pl.BlockSpec(memory_space=pltpu.HBM)],
        out_specs=vmem(),
        scratch_shapes=[pltpu.VMEM((STATIONS, 8, LANES), BF16), pltpu.SemaphoreType.DMA((COPIES,))],
        name="cut_chunk",
        **kw,
    )(screens)


def pick_near_kernel(roots, in_ref, out_ref):
    for s in range(SLOTS):
        piece = in_ref[roots[s] // FAR]
        for k in range(FAR):
            out_ref[k, s] = piece


def pick_near(roots, pieces, **kw):
    return pl.pallas_call(
        pick_near_kernel,
        out_shape=jax.ShapeDtypeStruct((FAR, SLOTS, 16, LANES), BF16),
        in_specs=[smem(), vmem()],
        out_specs=vmem(),
        name="pick_near",
        compiler_params=room(),
        **kw,
    )(roots, pieces)


def pick_far_kernel(roots, in_ref, out_ref):
    pieces = [in_ref[roots[s] % FAR, s].astype(F32) for s in range(SLOTS)]
    rows = jnp.concatenate(
        [pieces[s][4 * i:4 * i + 4] for i in range(ST_PIECE) for s in range(SLOTS)], axis=0
    ).astype(BF16)
    for j in range(NEAR):
        out_ref[j] = rows


def pick_far(roots, pieces, **kw):
    return pl.pallas_call(
        pick_far_kernel,
        out_shape=jax.ShapeDtypeStruct((NEAR, ST_PIECE * SLOTS * 4, LANES), BF16),
        in_specs=[smem(), vmem()],
        out_specs=vmem(),
        name="pick_far",
        compiler_params=room(),
        **kw,
    )(roots, pieces)


ROWS_ST = SLOTS * 4


def asked_kernel(meta, in_ref, out_ref, table, stage):
    for z in range(NEAR):
        wide = in_ref[z].astype(F32)
        for i in range(ST_PIECE):
            table[z * ST_PIECE + i, 0:ROWS_ST, :] = wide[ROWS_ST * i:ROWS_ST * (i + 1)]

    @pl.loop(0, PEERS)
    def _(t):
        for r in range(REQS):
            station = meta[t * META + PAIR_LANE + r]
            stage[ROWS_ST * r:ROWS_ST * (r + 1), :] = table[station, 0:ROWS_ST, :]
        out_ref[t] = stage[...].astype(BF16)


def asked(meta, pieces, **kw):
    return pl.pallas_call(
        asked_kernel,
        out_shape=jax.ShapeDtypeStruct((PEERS, REQS * ROWS_ST, LANES), BF16),
        in_specs=[smem(), vmem()],
        out_specs=vmem(),
        scratch_shapes=[
            pltpu.VMEM((STATIONS, 16, LANES), F32),
            pltpu.VMEM((REQS * ROWS_ST, LANES), F32),
        ],
        name="asked_stations",
        cost_estimate=pl.CostEstimate(flops=1000000, bytes_accessed=600000, transcendentals=0),
        compiler_params=room(),
        **kw,
    )(meta, pieces)


def screen_kernel(x_ref, in_ref, out_ref, wide, tmp):
    rows = REQS * ROWS_ST
    for t in range(PEERS):
        wide[rows * t:rows * (t + 1), :] = in_ref[t].astype(F32)

    def entry(request, slot, p, half):
        start = half * rows + request * ROWS_ST + slot * 4 + p
        return wide[pl.ds(start, 8, stride=2 * rows), :]

    def product(first, second):
        result = []
        for i in range(2):
            for j in range(2):
                one = times(first[2 * i], second[j])
                two = times(first[2 * i + 1], second[2 + j])
                result.append((one[0] + two[0], one[1] + two[1]))
        return result

    for sub in range(SUBS):
        total = None
        for slot in range(SLOTS):
            first = [(entry(2 * sub, slot, p, 0), entry(2 * sub, slot, p, 1)) for p in range(4)]
            second = [(entry(2 * sub + 1, slot, p, 0), -entry(2 * sub + 1, slot, p, 1)) for p in (0, 2, 1, 3)]
            key = slot * SUBS + sub
            image = [(x_ref[key, p], x_ref[key, 4 + p]) for p in range(4)]
            part = product(product(first, image), second)
            if total is None:
                total = part
            else:
                total = [(a[0] + b[0], a[1] + b[1]) for a, b in zip(total, part)]
        for p in range(4):
            tmp[8 * p:8 * p + 8, :] = total[p][0]
            tmp[32 + 8 * p:40 + 8 * p, :] = total[p][1]
        for a in range(8):
            out_ref[0, sub, :, LANES * a:LANES * (a + 1)] = tmp[pl.ds(a, 8, stride=8), :]


def screen_product(x, screens, **kw):
    return pl.pallas_call(
        screen_kernel,
        out_shape=jax.ShapeDtypeStruct((1, SUBS, 8, SIDE * SIDE), F32),
        in_specs=[vmem(), vmem()],
        out_specs=vmem(),
        scratch_shapes=[
            pltpu.VMEM((PEERS * REQS * ROWS_ST, LANES), F32),
            pltpu.VMEM((64, LANES), F32),
        ],
        name="screen_product",
        cost_estimate=pl.CostEstimate(flops=3000000, bytes_accessed=1000000, transcendentals=0),
        compiler_params=room(),
        **kw,
    )(x, screens)


def meta_of(arrived):
    return arrived[:, META_ROW, :META].astype(jnp.int32).reshape(-1)


def on_device(visibility, coordinate, block_count, owner_index, subgrid_index, offsets,
              station_pair, screens, slot_owner):
    near = [[k * FAR + j for k in range(NEAR)] for j in range(FAR)]
    far = [[k * FAR + j for j in range(FAR)] for k in range(NEAR)]

    def exchange(array, axis, groups=None):
        return lax.all_to_all(array, axis, 0, 0, axis_index_groups=groups, tiled=True)

    pieces = exchange(chunk_of(screens), "uv", near)
    sent = pack(owner_index[..., 0], subgrid_index, block_count, station_pair.swapaxes(1, 2), visibility, coordinate)
    pieces, sent = lax.optimization_barrier((pieces, sent))
    pieces = exchange(pick_near(slot_owner, pieces), "uv", far)
    pieces, sent = lax.optimization_barrier((pieces, sent))
    arrived = exchange(sent, "tm")
    meta = meta_of(arrived)
    pieces = exchange(pick_far(slot_owner, pieces), "uv", near)
    x = grid_blocks(meta, offsets.swapaxes(1, 2), arrived)
    meta, x = lax.optimization_barrier((meta, x))
    wanted = exchange(asked(meta, pieces), "tm")
    return screen_product(x, wanted)


def solution(mesh):
    placed = (
        P(None, "uv", "tm", None, None),
        P(None, "uv", "tm", None, None),
        P(None, "uv", "tm"),
        P(None, "uv", "tm", None),
        P(None, "uv", "tm"),
        P("uv", "tm", None),
        P("uv", "tm", None),
        P("uv", None, None, None),
        P(),
    )
    return jax.shard_map(
        on_device, mesh=mesh, in_specs=placed, out_specs=P("uv", "tm", None, None), check_vma=False
    )
```

```python
import jax
import jax.numpy as jnp
from jax import lax
from jax.experimental import pallas as pl
from jax.experimental.pallas import tpu as pltpu
from jax.sharding import PartitionSpec as P

SLOTS = 3
SIDE = 32
BLOCKS = 16
PEERS = 16
CAP = 2
SUBS = 4
STATIONS = 64
PER = SLOTS * CAP
NEAR = 16
FAR = 4
ST_PIECE = STATIONS // NEAR
REQS = 2 * SUBS
LANES = 128
F32 = jnp.float32
BF16 = jnp.bfloat16

ROWS = 64
U_ROW = PER * 8
V_ROW = U_ROW + PER
META_ROW = V_ROW + PER
META = 32
PAIR_LANE = 16

COS_POLY = (1.0, -19.73920440673828, 64.93911743164062, -85.45014190673828, 60.167633056640625,
            -25.967601776123047, 6.528658866882324)
SIN_POLY = (6.283185005187988, -41.341590881347656, 81.59994506835938, -76.6144790649414,
            41.34288787841797, -12.471244812011719)


def smem():
    return pl.BlockSpec(memory_space=pltpu.SMEM)


def vmem():
    return pl.BlockSpec(memory_space=pltpu.VMEM)


def room():
    return pltpu.CompilerParams(vmem_limit_bytes=8 * 1024 * 1024)


def horner(x, poly):
    total = jnp.full_like(x, poly[-1])
    for coefficient in poly[-2::-1]:
        total = total * x + coefficient
    return total


def cis(turns):
    part = turns - jnp.floor(turns + 0.5)
    square = part * part
    return horner(square, COS_POLY), horner(square, SIN_POLY) * part


def times(a, b):
    return a[0] * b[0] - a[1] * b[1], a[0] * b[1] + a[1] * b[0]


def pack_kernel(owners, subs, counts, pair, vis_ref, coord_ref, out_ref, taken, stage):
    lane = lax.broadcasted_iota(jnp.int32, (1, LANES), 1)
    pairs = jnp.zeros((1, LANES), F32)
    for j in range(REQS):
        pairs = jnp.where(lane == PAIR_LANE + j, pair[0, j % 2, j // 2].astype(F32), pairs)
    last = lax.broadcasted_iota(jnp.int32, (8, LANES), 0) == META_ROW % 8
    last = jnp.where(last, pairs, 0.0)

    @pl.loop(0, PEERS)
    def _(o):
        stage[o, 0:ROWS - 16, :] = jnp.zeros((ROWS - 16, LANES), F32)
        for half in (16, 8):
            first = ROWS - half
            stage[o, first:first + 8, :] = last if META_ROW // 8 * 8 == first else jnp.zeros_like(last)

    for slot in range(SLOTS):
        for o in range(PEERS):
            taken[o] = 0

        @pl.loop(0, BLOCKS)
        def _(i):
            owner = owners[slot, 0, i]
            rank = taken[owner]
            taken[owner] = rank + 1
            k = slot * CAP + rank
            values = vis_ref[slot, 0, i].astype(F32)
            values = jnp.where(lane < counts[slot, 0, i], values, 0.0)
            stage[owner, pl.ds(pl.multiple_of(k * 8, 8), 8), :] = values
            where = coord_ref[slot, 0, i].astype(F32)
            stage[owner, pl.ds(U_ROW + k, 1), :] = where[0:1]
            stage[owner, pl.ds(V_ROW + k, 1), :] = where[1:2]
            meta = jnp.where(lane == 2 * k, subs[slot, 0, i].astype(F32), jnp.where(lane == 2 * k + 1, 1.0, 0.0))
            stage[owner, META_ROW:META_ROW + 1, :] += meta

    @pl.loop(0, PEERS)
    def _(o):
        out_ref[o] = stage[o].astype(BF16)


def pack(owners, subs, counts, pair, visibility, coordinate, **kw):
    return pl.pallas_call(
        pack_kernel,
        out_shape=jax.ShapeDtypeStruct((PEERS, ROWS, LANES), BF16),
        in_specs=[smem()] * 4 + [vmem(), vmem()],
        out_specs=vmem(),
        scratch_shapes=[pltpu.SMEM((PEERS,), jnp.int32), pltpu.VMEM((PEERS, ROWS, LANES), F32)],
        name="pack_blocks",
        cost_estimate=pl.CostEstimate(flops=2000000, bytes_accessed=600000, transcendentals=0),
        compiler_params=room(),
        **kw,
    )(owners, subs, counts, pair, visibility, coordinate)


def block_transpose(rows):
    lane = lax.broadcasted_iota(jnp.int32, (8, LANES), 1)
    rows = list(rows)
    for bit in range(2):
        step = SIDE << bit
        upper = (lane & step) != 0
        for low in range(4):
            if low >> bit & 1:
                continue
            high = low | 1 << bit
            x, y = rows[low], rows[high]
            rows[low] = jnp.where(upper, pltpu.roll(y, step, 1), x)
            rows[high] = jnp.where(upper, y, pltpu.roll(x, LANES - step, 1))
    return rows


BATCH = 4


def grid_kernel(meta, offs, rows_ref, x_ref, acc, coords, order, bucket):
    acc[...] = jnp.zeros_like(acc)
    for t in range(PEERS):
        coords[t] = rows_ref[t, ROWS - 16:ROWS, :].astype(F32)

    def gather(t, carry):
        count, spare = carry
        for k in range(PER):
            b = t * PER + k
            sub = meta[t * META + 2 * k]
            live = meta[t * META + 2 * k + 1]
            order[count] = b
            bucket[count] = (k // CAP) * SUBS + sub
            spare = jnp.where(live == 0, b, spare)
            count = count + live
        return count, spare

    count, spare = lax.fori_loop(0, PEERS, gather, (jnp.int32(0), jnp.int32(0)))
    for j in range(BATCH):
        order[count + j] = spare
        bucket[count + j] = 0

    sublane = lax.broadcasted_iota(jnp.int32, (8, LANES), 0).astype(F32)
    seed_l = (sublane * 4.0 - 16.0) * (1.0 / SIDE)
    seed_m = (sublane - 16.0) * (1.0 / SIDE)

    @pl.loop(0, (count + (BATCH - 1)) // BATCH)
    def _(step):
        for j in range(BATCH):
            b = order[step * BATCH + j]
            key = bucket[step * BATCH + j]
            sub = key % SUBS
            t = b // PER
            k = b % PER
            tile = rows_ref[t, pl.ds(pl.multiple_of(k // CAP * 16, 16), 16), :].astype(F32)
            tile = jnp.where(k % CAP == 0, tile[0:8], tile[8:16])
            u = coords[t, pl.ds(U_ROW - (ROWS - 16) + k, 1), :]
            v = coords[t, pl.ds(V_ROW - (ROWS - 16) + k, 1), :]
            du = jnp.broadcast_to(u - offs[0, 0, sub].astype(F32), (8, LANES))
            dv = jnp.broadcast_to(v - offs[0, 1, sub].astype(F32), (8, LANES))
            turn_l = cis(du * (1.0 / SIDE))
            turn_m = cis(dv * (8.0 / SIDE))
            current = cis(du * seed_l)
            cos_rows, sin_rows = [current[0]], [current[1]]
            for _ in range(3):
                current = times(current, turn_l)
                cos_rows.append(current[0])
                sin_rows.append(current[1])
            left = jnp.concatenate(cos_rows + sin_rows, axis=0).astype(BF16)
            phase = [cis(dv * seed_m)]
            for _ in range(3):
                phase.append(times(phase[-1], turn_m))
            real_rows, imag_rows = [], []
            for p in range(4):
                vis = tile[p:p + 1, :], tile[4 + p:5 + p, :]
                for m in range(4):
                    real, imag = times(vis, phase[m])
                    real_rows.append(real)
                    imag_rows.append(imag)
            right = jnp.concatenate(real_rows + imag_rows, axis=0).astype(BF16)
            acc[key] += lax.dot_general(
                left, right, (((1,), (1,)), ((), ())), preferred_element_type=F32
            )

    @pl.loop(0, SLOTS * SUBS)
    def _(key):
        upper = acc[key, 0:SIDE, :]
        lower = acc[key, SIDE:2 * SIDE, :]
        real = upper[:, :LANES] - lower[:, LANES:]
        imag = upper[:, LANES:] + lower[:, :LANES]
        for part, image in enumerate((real, imag)):
            for p, plane in enumerate(block_transpose([image[8 * b:8 * b + 8] for b in range(4)])):
                x_ref[key, 4 * part + p] = plane


def grid_blocks(meta, offs, rows, **kw):
    return pl.pallas_call(
        grid_kernel,
        out_shape=jax.ShapeDtypeStruct((SLOTS * SUBS, 8, 8, LANES), F32),
        in_specs=[smem(), smem(), vmem()],
        out_specs=vmem(),
        scratch_shapes=[
            pltpu.VMEM((SLOTS * SUBS, 2 * SIDE, 8 * SIDE), F32),
            pltpu.VMEM((PEERS, 16, LANES), F32),
            pltpu.SMEM((PEERS * PER + BATCH,), jnp.int32),
            pltpu.SMEM((PEERS * PER + BATCH,), jnp.int32),
        ],
        name="grid_blocks",
        cost_estimate=pl.CostEstimate(flops=800000000, bytes_accessed=800000, transcendentals=0),
        compiler_params=room(),
        **kw,
    )(meta, offs, rows)


COPIES = 4


def chunk_kernel(screens_ref, out_ref, in_ref, arrived):
    t = lax.axis_index("tm")
    lanes = pl.ds(pl.multiple_of(t // 2 * LANES, LANES), LANES)
    share = STATIONS // COPIES
    copies = []
    for c in range(COPIES):
        some = pl.ds(c * share, share)
        copies.append(pltpu.make_async_copy(screens_ref.at[0, some, :, lanes], in_ref.at[some], arrived.at[c]))
        copies[-1].start()
    odd = t % 2 == 1
    low = lax.broadcasted_iota(jnp.int32, (8, LANES), 0) < 4

    def two(first, second):
        a, b = in_ref[first].astype(F32), in_ref[second].astype(F32)
        a, b = jnp.where(odd, pltpu.roll(a, 4, 0), a), jnp.where(odd, b, pltpu.roll(b, 4, 0))
        return jnp.where(low, a, b)

    for j in range(NEAR):
        first = j * ST_PIECE
        if first % share == 0:
            copies[first // share].wait()
        out_ref[j] = jnp.concatenate([two(first, first + 1), two(first + 2, first + 3)], axis=0).astype(BF16)


def chunk_of(screens, **kw):
    return pl.pallas_call(
        chunk_kernel,
        out_shape=jax.ShapeDtypeStruct((NEAR, ST_PIECE * 4, LANES), BF16),
        in_specs=[pl.BlockSpec(memory_space=pltpu.HBM)],
        out_specs=vmem(),
        scratch_shapes=[pltpu.VMEM((STATIONS, 8, LANES), BF16), pltpu.SemaphoreType.DMA((COPIES,))],
        name="cut_chunk",
        **kw,
    )(screens)


def pick_near_kernel(roots, in_ref, out_ref):
    for s in range(SLOTS):
        out_ref[s] = in_ref[roots[s] // FAR]


def pick_near(roots, pieces, **kw):
    return pl.pallas_call(
        pick_near_kernel,
        out_shape=jax.ShapeDtypeStruct((SLOTS, 16, LANES), BF16),
        in_specs=[smem(), vmem()],
        out_specs=vmem(),
        name="pick_near",
        compiler_params=room(),
        **kw,
    )(roots, pieces)


def pick_far_kernel(roots, even_ref, odd_ref, out_ref):
    me = lax.axis_index("uv")
    pieces = []
    for s in range(SLOTS):
        shift = (me - roots[s] + FAR * NEAR) % FAR
        k = shift // 2 * SLOTS + s
        pieces.append(jnp.where(shift % 2 == 0, even_ref[k].astype(F32), odd_ref[k].astype(F32)))
    rows = jnp.concatenate(
        [pieces[s][4 * i:4 * i + 4] for i in range(ST_PIECE) for s in range(SLOTS)], axis=0
    ).astype(BF16)
    for j in range(NEAR):
        out_ref[j] = rows


def pick_far(roots, even, odd, **kw):
    return pl.pallas_call(
        pick_far_kernel,
        out_shape=jax.ShapeDtypeStruct((NEAR, ST_PIECE * SLOTS * 4, LANES), BF16),
        in_specs=[smem(), vmem(), vmem()],
        out_specs=vmem(),
        name="pick_far",
        cost_estimate=pl.CostEstimate(flops=4200000000, bytes_accessed=800000, transcendentals=0),
        compiler_params=room(),
        **kw,
    )(roots, even, odd)


ROWS_ST = SLOTS * 4


def asked_kernel(meta, in_ref, out_ref, table, stage):
    for z in range(NEAR):
        wide = in_ref[z].astype(F32)
        for i in range(ST_PIECE):
            table[z * ST_PIECE + i, 0:ROWS_ST, :] = wide[ROWS_ST * i:ROWS_ST * (i + 1)]

    @pl.loop(0, PEERS)
    def _(t):
        for r in range(REQS):
            station = meta[t * META + PAIR_LANE + r]
            stage[ROWS_ST * r:ROWS_ST * (r + 1), :] = table[station, 0:ROWS_ST, :]
        out_ref[t] = stage[...].astype(BF16)


def asked(meta, pieces, **kw):
    return pl.pallas_call(
        asked_kernel,
        out_shape=jax.ShapeDtypeStruct((PEERS, REQS * ROWS_ST, LANES), BF16),
        in_specs=[smem(), vmem()],
        out_specs=vmem(),
        scratch_shapes=[
            pltpu.VMEM((STATIONS, 16, LANES), F32),
            pltpu.VMEM((REQS * ROWS_ST, LANES), F32),
        ],
        name="asked_stations",
        cost_estimate=pl.CostEstimate(flops=1000000, bytes_accessed=600000, transcendentals=0),
        compiler_params=room(),
        **kw,
    )(meta, pieces)


def screen_kernel(x_ref, in_ref, out_ref, wide, tmp):
    rows = REQS * ROWS_ST
    for t in range(PEERS):
        wide[rows * t:rows * (t + 1), :] = in_ref[t].astype(F32)

    def entry(request, slot, p, half):
        start = half * rows + request * ROWS_ST + slot * 4 + p
        return wide[pl.ds(start, 8, stride=2 * rows), :]

    def product(first, second):
        result = []
        for i in range(2):
            for j in range(2):
                one = times(first[2 * i], second[j])
                two = times(first[2 * i + 1], second[2 + j])
                result.append((one[0] + two[0], one[1] + two[1]))
        return result

    for sub in range(SUBS):
        total = None
        for slot in range(SLOTS):
            first = [(entry(2 * sub, slot, p, 0), entry(2 * sub, slot, p, 1)) for p in range(4)]
            second = [(entry(2 * sub + 1, slot, p, 0), -entry(2 * sub + 1, slot, p, 1)) for p in (0, 2, 1, 3)]
            key = slot * SUBS + sub
            image = [(x_ref[key, p], x_ref[key, 4 + p]) for p in range(4)]
            part = product(product(first, image), second)
            if total is None:
                total = part
            else:
                total = [(a[0] + b[0], a[1] + b[1]) for a, b in zip(total, part)]
        for p in range(4):
            tmp[8 * p:8 * p + 8, :] = total[p][0]
            tmp[32 + 8 * p:40 + 8 * p, :] = total[p][1]
        for a in range(8):
            out_ref[0, sub, :, LANES * a:LANES * (a + 1)] = tmp[pl.ds(a, 8, stride=8), :]


def screen_product(x, screens, **kw):
    return pl.pallas_call(
        screen_kernel,
        out_shape=jax.ShapeDtypeStruct((1, SUBS, 8, SIDE * SIDE), F32),
        in_specs=[vmem(), vmem()],
        out_specs=vmem(),
        scratch_shapes=[
            pltpu.VMEM((PEERS * REQS * ROWS_ST, LANES), F32),
            pltpu.VMEM((64, LANES), F32),
        ],
        name="screen_product",
        cost_estimate=pl.CostEstimate(flops=3000000, bytes_accessed=1000000, transcendentals=0),
        compiler_params=room(),
        **kw,
    )(x, screens)


def meta_of(arrived):
    return arrived[:, META_ROW, :META].astype(jnp.int32).reshape(-1)


def on_device(visibility, coordinate, block_count, owner_index, subgrid_index, offsets,
              station_pair, screens, slot_owner):
    near = [[k * FAR + j for k in range(NEAR)] for j in range(FAR)]

    def shifted(array, shift):
        pairs = [(k * FAR + j, k * FAR + (j + shift) % FAR) for k in range(NEAR) for j in range(FAR)]
        return lax.ppermute(array, "uv", pairs)

    def exchange(array, axis, groups=None):
        return lax.all_to_all(array, axis, 0, 0, axis_index_groups=groups, tiled=True)

    pieces = exchange(chunk_of(screens), "uv", near)
    sent = pack(owner_index[..., 0], subgrid_index, block_count, station_pair.swapaxes(1, 2), visibility, coordinate)
    pieces, sent = lax.optimization_barrier((pieces, sent))
    piece = pick_near(slot_owner, pieces)
    even = jnp.concatenate([piece, shifted(piece, 2)], axis=0)
    odd = shifted(even, 1)
    arrived = exchange(sent, "tm")
    meta = meta_of(arrived)
    pieces = exchange(pick_far(slot_owner, even, odd), "uv", near)
    x = grid_blocks(meta, offsets.swapaxes(1, 2), arrived)
    meta, x = lax.optimization_barrier((meta, x))
    wanted = exchange(asked(meta, pieces), "tm")
    return screen_product(x, wanted)


def solution(mesh):
    placed = (
        P(None, "uv", "tm", None, None),
        P(None, "uv", "tm", None, None),
        P(None, "uv", "tm"),
        P(None, "uv", "tm", None),
        P(None, "uv", "tm"),
        P("uv", "tm", None),
        P("uv", "tm", None),
        P("uv", None, None, None),
        P(),
    )
    return jax.shard_map(
        on_device, mesh=mesh, in_specs=placed, out_specs=P("uv", "tm", None, None), check_vma=False
    )
```

```python
import jax
import jax.numpy as jnp
from jax import lax
from jax.experimental import pallas as pl
from jax.experimental.pallas import tpu as pltpu
from jax.sharding import PartitionSpec as P

SLOTS = 3
SIDE = 32
BLOCKS = 16
PEERS = 16
CAP = 2
SUBS = 4
STATIONS = 64
PER = SLOTS * CAP
NEAR = 16
FAR = 4
ST_PIECE = STATIONS // NEAR
REQS = 2 * SUBS
LANES = 128
F32 = jnp.float32
BF16 = jnp.bfloat16

ROWS = 64
U_ROW = PER * 8
V_ROW = U_ROW + PER
META_ROW = V_ROW + PER
META = 32
PAIR_LANE = 16

COS_POLY = (1.0, -19.73920440673828, 64.93911743164062, -85.45014190673828, 60.167633056640625,
            -25.967601776123047, 6.528658866882324)
SIN_POLY = (6.283185005187988, -41.341590881347656, 81.59994506835938, -76.6144790649414,
            41.34288787841797, -12.471244812011719)


def smem():
    return pl.BlockSpec(memory_space=pltpu.SMEM)


def vmem():
    return pl.BlockSpec(memory_space=pltpu.VMEM)


def room():
    return pltpu.CompilerParams(vmem_limit_bytes=8 * 1024 * 1024)


def horner(x, poly):
    total = jnp.full_like(x, poly[-1])
    for coefficient in poly[-2::-1]:
        total = total * x + coefficient
    return total


def cis(turns):
    part = turns - jnp.floor(turns + 0.5)
    square = part * part
    return horner(square, COS_POLY), horner(square, SIN_POLY) * part


def times(a, b):
    return a[0] * b[0] - a[1] * b[1], a[0] * b[1] + a[1] * b[0]


def pack_kernel(owners, subs, counts, pair, vis_ref, coord_ref, out_ref, taken, stage):
    lane = lax.broadcasted_iota(jnp.int32, (1, LANES), 1)
    pairs = jnp.zeros((1, LANES), F32)
    for j in range(REQS):
        pairs = jnp.where(lane == PAIR_LANE + j, pair[0, j % 2, j // 2].astype(F32), pairs)
    last = lax.broadcasted_iota(jnp.int32, (8, LANES), 0) == META_ROW % 8
    last = jnp.where(last, pairs, 0.0)

    @pl.loop(0, PEERS)
    def _(o):
        stage[o, 0:ROWS - 16, :] = jnp.zeros((ROWS - 16, LANES), F32)
        for half in (16, 8):
            first = ROWS - half
            stage[o, first:first + 8, :] = last if META_ROW // 8 * 8 == first else jnp.zeros_like(last)

    for slot in range(SLOTS):
        for o in range(PEERS):
            taken[o] = 0

        @pl.loop(0, BLOCKS)
        def _(i):
            owner = owners[slot, 0, i]
            rank = taken[owner]
            taken[owner] = rank + 1
            k = slot * CAP + rank
            values = vis_ref[slot, 0, i].astype(F32)
            values = jnp.where(lane < counts[slot, 0, i], values, 0.0)
            stage[owner, pl.ds(pl.multiple_of(k * 8, 8), 8), :] = values
            where = coord_ref[slot, 0, i].astype(F32)
            stage[owner, pl.ds(U_ROW + k, 1), :] = where[0:1]
            stage[owner, pl.ds(V_ROW + k, 1), :] = where[1:2]
            meta = jnp.where(lane == 2 * k, subs[slot, 0, i].astype(F32), jnp.where(lane == 2 * k + 1, 1.0, 0.0))
            stage[owner, META_ROW:META_ROW + 1, :] += meta

    @pl.loop(0, PEERS)
    def _(o):
        out_ref[o] = stage[o].astype(BF16)


def pack(owners, subs, counts, pair, visibility, coordinate, **kw):
    return pl.pallas_call(
        pack_kernel,
        out_shape=jax.ShapeDtypeStruct((PEERS, ROWS, LANES), BF16),
        in_specs=[smem()] * 4 + [vmem(), vmem()],
        out_specs=vmem(),
        scratch_shapes=[pltpu.SMEM((PEERS,), jnp.int32), pltpu.VMEM((PEERS, ROWS, LANES), F32)],
        name="pack_blocks",
        cost_estimate=pl.CostEstimate(flops=2000000, bytes_accessed=600000, transcendentals=0),
        compiler_params=room(),
        **kw,
    )(owners, subs, counts, pair, visibility, coordinate)


def block_transpose(rows):
    lane = lax.broadcasted_iota(jnp.int32, (8, LANES), 1)
    rows = list(rows)
    for bit in range(2):
        step = SIDE << bit
        upper = (lane & step) != 0
        for low in range(4):
            if low >> bit & 1:
                continue
            high = low | 1 << bit
            x, y = rows[low], rows[high]
            rows[low] = jnp.where(upper, pltpu.roll(y, step, 1), x)
            rows[high] = jnp.where(upper, y, pltpu.roll(x, LANES - step, 1))
    return rows


BATCH = 4


def grid_kernel(meta, offs, rows_ref, x_ref, acc, coords, order, bucket):
    acc[...] = jnp.zeros_like(acc)
    for t in range(PEERS):
        coords[t] = rows_ref[t, ROWS - 16:ROWS, :].astype(F32)

    def gather(t, carry):
        count, spare = carry
        for k in range(PER):
            b = t * PER + k
            sub = meta[t * META + 2 * k]
            live = meta[t * META + 2 * k + 1]
            order[count] = b
            bucket[count] = (k // CAP) * SUBS + sub
            spare = jnp.where(live == 0, b, spare)
            count = count + live
        return count, spare

    count, spare = lax.fori_loop(0, PEERS, gather, (jnp.int32(0), jnp.int32(0)))
    for j in range(BATCH):
        order[count + j] = spare
        bucket[count + j] = 0

    sublane = lax.broadcasted_iota(jnp.int32, (8, LANES), 0).astype(F32)
    seed_l = (sublane * 4.0 - 16.0) * (1.0 / SIDE)
    seed_m = (sublane - 16.0) * (1.0 / SIDE)

    @pl.loop(0, (count + (BATCH - 1)) // BATCH)
    def _(step):
        for j in range(BATCH):
            b = order[step * BATCH + j]
            key = bucket[step * BATCH + j]
            sub = key % SUBS
            t = b // PER
            k = b % PER
            tile = rows_ref[t, pl.ds(pl.multiple_of(k // CAP * 16, 16), 16), :].astype(F32)
            tile = jnp.where(k % CAP == 0, tile[0:8], tile[8:16])
            u = coords[t, pl.ds(U_ROW - (ROWS - 16) + k, 1), :]
            v = coords[t, pl.ds(V_ROW - (ROWS - 16) + k, 1), :]
            du = jnp.broadcast_to(u - offs[0, 0, sub].astype(F32), (8, LANES))
            dv = jnp.broadcast_to(v - offs[0, 1, sub].astype(F32), (8, LANES))
            turn_l = cis(du * (1.0 / SIDE))
            turn_m = cis(dv * (8.0 / SIDE))
            current = cis(du * seed_l)
            cos_rows, sin_rows = [current[0]], [current[1]]
            for _ in range(3):
                current = times(current, turn_l)
                cos_rows.append(current[0])
                sin_rows.append(current[1])
            left = jnp.concatenate(cos_rows + sin_rows, axis=0).astype(BF16)
            phase = [cis(dv * seed_m)]
            for _ in range(3):
                phase.append(times(phase[-1], turn_m))
            real_rows, imag_rows = [], []
            for p in range(4):
                vis = tile[p:p + 1, :], tile[4 + p:5 + p, :]
                for m in range(4):
                    real, imag = times(vis, phase[m])
                    real_rows.append(real)
                    imag_rows.append(imag)
            right = jnp.concatenate(real_rows + imag_rows, axis=0).astype(BF16)
            acc[key] += lax.dot_general(
                left, right, (((1,), (1,)), ((), ())), preferred_element_type=F32
            )

    @pl.loop(0, SLOTS * SUBS)
    def _(key):
        upper = acc[key, 0:SIDE, :]
        lower = acc[key, SIDE:2 * SIDE, :]
        real = upper[:, :LANES] - lower[:, LANES:]
        imag = upper[:, LANES:] + lower[:, :LANES]
        for part, image in enumerate((real, imag)):
            for p, plane in enumerate(block_transpose([image[8 * b:8 * b + 8] for b in range(4)])):
                x_ref[key, 4 * part + p] = plane


def grid_blocks(meta, offs, rows, **kw):
    return pl.pallas_call(
        grid_kernel,
        out_shape=jax.ShapeDtypeStruct((SLOTS * SUBS, 8, 8, LANES), F32),
        in_specs=[smem(), smem(), vmem()],
        out_specs=vmem(),
        scratch_shapes=[
            pltpu.VMEM((SLOTS * SUBS, 2 * SIDE, 8 * SIDE), F32),
            pltpu.VMEM((PEERS, 16, LANES), F32),
            pltpu.SMEM((PEERS * PER + BATCH,), jnp.int32),
            pltpu.SMEM((PEERS * PER + BATCH,), jnp.int32),
        ],
        name="grid_blocks",
        cost_estimate=pl.CostEstimate(flops=800000000, bytes_accessed=800000, transcendentals=0),
        compiler_params=room(),
        **kw,
    )(meta, offs, rows)


COPIES = 4


def chunk_kernel(screens_ref, out_ref, in_ref, arrived):
    t = lax.axis_index("tm")
    lanes = pl.ds(pl.multiple_of(t // 2 * LANES, LANES), LANES)
    share = STATIONS // COPIES
    copies = []
    for c in range(COPIES):
        some = pl.ds(c * share, share)
        copies.append(pltpu.make_async_copy(screens_ref.at[0, some, :, lanes], in_ref.at[some], arrived.at[c]))
        copies[-1].start()
    odd = t % 2 == 1
    low = lax.broadcasted_iota(jnp.int32, (8, LANES), 0) < 4

    def two(first, second):
        a, b = in_ref[first].astype(F32), in_ref[second].astype(F32)
        a, b = jnp.where(odd, pltpu.roll(a, 4, 0), a), jnp.where(odd, b, pltpu.roll(b, 4, 0))
        return jnp.where(low, a, b)

    for j in range(NEAR):
        first = j * ST_PIECE
        if first % share == 0:
            copies[first // share].wait()
        out_ref[j] = jnp.concatenate([two(first, first + 1), two(first + 2, first + 3)], axis=0).astype(BF16)


def chunk_of(screens, **kw):
    return pl.pallas_call(
        chunk_kernel,
        out_shape=jax.ShapeDtypeStruct((NEAR, ST_PIECE * 4, LANES), BF16),
        in_specs=[pl.BlockSpec(memory_space=pltpu.HBM)],
        out_specs=vmem(),
        scratch_shapes=[pltpu.VMEM((STATIONS, 8, LANES), BF16), pltpu.SemaphoreType.DMA((COPIES,))],
        name="cut_chunk",
        **kw,
    )(screens)


def pick_near_kernel(roots, in_ref, out_ref):
    for s in range(SLOTS):
        out_ref[s] = in_ref[roots[s] // FAR]


def pick_near(roots, pieces, **kw):
    return pl.pallas_call(
        pick_near_kernel,
        out_shape=jax.ShapeDtypeStruct((SLOTS, 16, LANES), BF16),
        in_specs=[smem(), vmem()],
        out_specs=vmem(),
        name="pick_near",
        compiler_params=room(),
        **kw,
    )(roots, pieces)


def pick_far_kernel(roots, even_ref, odd_ref, out_ref, rows, sent):
    me = lax.axis_index("uv")
    pieces = []
    for s in range(SLOTS):
        shift = (me - roots[s] + FAR * NEAR) % FAR
        k = shift // 2 * SLOTS + s
        pieces.append(jnp.where(shift % 2 == 0, even_ref[k].astype(F32), odd_ref[k].astype(F32)))
    rows[...] = jnp.concatenate(
        [pieces[s][4 * i:4 * i + 4] for i in range(ST_PIECE) for s in range(SLOTS)], axis=0
    ).astype(BF16)
    copies = [pltpu.make_async_copy(rows, out_ref.at[j], sent.at[j]) for j in range(NEAR)]
    for copy in copies:
        copy.start()
    for copy in copies:
        copy.wait()


def pick_far(roots, even, odd, **kw):
    return pl.pallas_call(
        pick_far_kernel,
        out_shape=jax.ShapeDtypeStruct((NEAR, ST_PIECE * SLOTS * 4, LANES), BF16),
        in_specs=[smem(), vmem(), vmem()],
        out_specs=pl.BlockSpec(memory_space=pltpu.HBM),
        scratch_shapes=[pltpu.VMEM((ST_PIECE * SLOTS * 4, LANES), BF16), pltpu.SemaphoreType.DMA((NEAR,))],
        name="pick_far",
        cost_estimate=pl.CostEstimate(flops=4200000000, bytes_accessed=800000, transcendentals=0),
        compiler_params=room(),
        **kw,
    )(roots, even, odd)


ROWS_ST = SLOTS * 4


def asked_kernel(meta, in_ref, out_ref, table, stage):
    for z in range(NEAR):
        wide = in_ref[z].astype(F32)
        for i in range(ST_PIECE):
            table[z * ST_PIECE + i, 0:ROWS_ST, :] = wide[ROWS_ST * i:ROWS_ST * (i + 1)]

    @pl.loop(0, PEERS)
    def _(t):
        for r in range(REQS):
            station = meta[t * META + PAIR_LANE + r]
            stage[ROWS_ST * r:ROWS_ST * (r + 1), :] = table[station, 0:ROWS_ST, :]
        out_ref[t] = stage[...].astype(BF16)


def asked(meta, pieces, **kw):
    return pl.pallas_call(
        asked_kernel,
        out_shape=jax.ShapeDtypeStruct((PEERS, REQS * ROWS_ST, LANES), BF16),
        in_specs=[smem(), vmem()],
        out_specs=vmem(),
        scratch_shapes=[
            pltpu.VMEM((STATIONS, 16, LANES), F32),
            pltpu.VMEM((REQS * ROWS_ST, LANES), F32),
        ],
        name="asked_stations",
        cost_estimate=pl.CostEstimate(flops=1000000, bytes_accessed=600000, transcendentals=0),
        compiler_params=room(),
        **kw,
    )(meta, pieces)


def screen_kernel(x_ref, in_ref, out_ref, wide, tmp):
    rows = REQS * ROWS_ST
    for t in range(PEERS):
        wide[rows * t:rows * (t + 1), :] = in_ref[t].astype(F32)

    def entry(request, slot, p, half):
        start = half * rows + request * ROWS_ST + slot * 4 + p
        return wide[pl.ds(start, 8, stride=2 * rows), :]

    def product(first, second):
        result = []
        for i in range(2):
            for j in range(2):
                one = times(first[2 * i], second[j])
                two = times(first[2 * i + 1], second[2 + j])
                result.append((one[0] + two[0], one[1] + two[1]))
        return result

    for sub in range(SUBS):
        total = None
        for slot in range(SLOTS):
            first = [(entry(2 * sub, slot, p, 0), entry(2 * sub, slot, p, 1)) for p in range(4)]
            second = [(entry(2 * sub + 1, slot, p, 0), -entry(2 * sub + 1, slot, p, 1)) for p in (0, 2, 1, 3)]
            key = slot * SUBS + sub
            image = [(x_ref[key, p], x_ref[key, 4 + p]) for p in range(4)]
            part = product(product(first, image), second)
            if total is None:
                total = part
            else:
                total = [(a[0] + b[0], a[1] + b[1]) for a, b in zip(total, part)]
        for p in range(4):
            tmp[8 * p:8 * p + 8, :] = total[p][0]
            tmp[32 + 8 * p:40 + 8 * p, :] = total[p][1]
        for a in range(8):
            out_ref[0, sub, :, LANES * a:LANES * (a + 1)] = tmp[pl.ds(a, 8, stride=8), :]


def screen_product(x, screens, **kw):
    return pl.pallas_call(
        screen_kernel,
        out_shape=jax.ShapeDtypeStruct((1, SUBS, 8, SIDE * SIDE), F32),
        in_specs=[vmem(), vmem()],
        out_specs=vmem(),
        scratch_shapes=[
            pltpu.VMEM((PEERS * REQS * ROWS_ST, LANES), F32),
            pltpu.VMEM((64, LANES), F32),
        ],
        name="screen_product",
        cost_estimate=pl.CostEstimate(flops=3000000, bytes_accessed=1000000, transcendentals=0),
        compiler_params=room(),
        **kw,
    )(x, screens)


def meta_of(arrived):
    return arrived[:, META_ROW, :META].astype(jnp.int32).reshape(-1)


def on_device(visibility, coordinate, block_count, owner_index, subgrid_index, offsets,
              station_pair, screens, slot_owner):
    near = [[k * FAR + j for k in range(NEAR)] for j in range(FAR)]

    def shifted(array, shift):
        pairs = [(k * FAR + j, k * FAR + (j + shift) % FAR) for k in range(NEAR) for j in range(FAR)]
        return lax.ppermute(array, "uv", pairs)

    def exchange(array, axis, groups=None):
        return lax.all_to_all(array, axis, 0, 0, axis_index_groups=groups, tiled=True)

    pieces = exchange(chunk_of(screens), "uv", near)
    sent = pack(owner_index[..., 0], subgrid_index, block_count, station_pair.swapaxes(1, 2), visibility, coordinate)
    pieces, sent = lax.optimization_barrier((pieces, sent))
    piece = pick_near(slot_owner, pieces)
    even = jnp.concatenate([piece, shifted(piece, 2)], axis=0)
    odd = shifted(even, 1)
    arrived = exchange(sent, "tm")
    meta = meta_of(arrived)
    pieces = exchange(pick_far(slot_owner, even, odd), "uv", near)
    x = grid_blocks(meta, offsets.swapaxes(1, 2), arrived)
    meta, x = lax.optimization_barrier((meta, x))
    wanted = exchange(asked(meta, pieces), "tm")
    return screen_product(x, wanted)


def solution(mesh):
    placed = (
        P(None, "uv", "tm", None, None),
        P(None, "uv", "tm", None, None),
        P(None, "uv", "tm"),
        P(None, "uv", "tm", None),
        P(None, "uv", "tm"),
        P("uv", "tm", None),
        P("uv", "tm", None),
        P("uv", None, None, None),
        P(),
    )
    return jax.shard_map(
        on_device, mesh=mesh, in_specs=placed, out_specs=P("uv", "tm", None, None), check_vma=False
    )
```

```python
import jax
import jax.numpy as jnp
from jax import lax
from jax.experimental import pallas as pl
from jax.experimental.pallas import tpu as pltpu
from jax.sharding import PartitionSpec as P

SLOTS = 3
SIDE = 32
BLOCKS = 16
PEERS = 16
CAP = 2
SUBS = 4
STATIONS = 64
PER = SLOTS * CAP
NEAR = 16
FAR = 4
ST_PIECE = STATIONS // NEAR
REQS = 2 * SUBS
LANES = 128
F32 = jnp.float32
BF16 = jnp.bfloat16

ROWS = 64
U_ROW = PER * 8
V_ROW = U_ROW + PER
META_ROW = V_ROW + PER
META = 32
PAIR_LANE = 16

COS_POLY = (1.0, -19.73920440673828, 64.93911743164062, -85.45014190673828, 60.167633056640625,
            -25.967601776123047, 6.528658866882324)
SIN_POLY = (6.283185005187988, -41.341590881347656, 81.59994506835938, -76.6144790649414,
            41.34288787841797, -12.471244812011719)


def smem():
    return pl.BlockSpec(memory_space=pltpu.SMEM)


def vmem():
    return pl.BlockSpec(memory_space=pltpu.VMEM)


def room():
    return pltpu.CompilerParams(vmem_limit_bytes=8 * 1024 * 1024)


def horner(x, poly):
    total = jnp.full_like(x, poly[-1])
    for coefficient in poly[-2::-1]:
        total = total * x + coefficient
    return total


def cis(turns):
    part = turns - jnp.floor(turns + 0.5)
    square = part * part
    return horner(square, COS_POLY), horner(square, SIN_POLY) * part


def times(a, b):
    return a[0] * b[0] - a[1] * b[1], a[0] * b[1] + a[1] * b[0]


def pack_kernel(owners, subs, counts, pair, vis_ref, coord_ref, out_ref, taken, stage):
    lane = lax.broadcasted_iota(jnp.int32, (1, LANES), 1)
    pairs = jnp.zeros((1, LANES), F32)
    for j in range(REQS):
        pairs = jnp.where(lane == PAIR_LANE + j, pair[0, j % 2, j // 2].astype(F32), pairs)
    last = lax.broadcasted_iota(jnp.int32, (8, LANES), 0) == META_ROW % 8
    last = jnp.where(last, pairs, 0.0)

    @pl.loop(0, PEERS)
    def _(o):
        stage[o, 0:ROWS - 16, :] = jnp.zeros((ROWS - 16, LANES), F32)
        for half in (16, 8):
            first = ROWS - half
            stage[o, first:first + 8, :] = last if META_ROW // 8 * 8 == first else jnp.zeros_like(last)

    for slot in range(SLOTS):
        for o in range(PEERS):
            taken[o] = 0

        @pl.loop(0, BLOCKS)
        def _(i):
            owner = owners[slot, 0, i]
            rank = taken[owner]
            taken[owner] = rank + 1
            k = slot * CAP + rank
            values = vis_ref[slot, 0, i].astype(F32)
            values = jnp.where(lane < counts[slot, 0, i], values, 0.0)
            stage[owner, pl.ds(pl.multiple_of(k * 8, 8), 8), :] = values
            where = coord_ref[slot, 0, i].astype(F32)
            stage[owner, pl.ds(U_ROW + k, 1), :] = where[0:1]
            stage[owner, pl.ds(V_ROW + k, 1), :] = where[1:2]
            meta = jnp.where(lane == 2 * k, subs[slot, 0, i].astype(F32), jnp.where(lane == 2 * k + 1, 1.0, 0.0))
            stage[owner, META_ROW:META_ROW + 1, :] += meta

    @pl.loop(0, PEERS)
    def _(o):
        out_ref[o] = stage[o].astype(BF16)


def pack(owners, subs, counts, pair, visibility, coordinate, **kw):
    return pl.pallas_call(
        pack_kernel,
        out_shape=jax.ShapeDtypeStruct((PEERS, ROWS, LANES), BF16),
        in_specs=[smem()] * 4 + [vmem(), vmem()],
        out_specs=vmem(),
        scratch_shapes=[pltpu.SMEM((PEERS,), jnp.int32), pltpu.VMEM((PEERS, ROWS, LANES), F32)],
        name="pack_blocks",
        cost_estimate=pl.CostEstimate(flops=2000000, bytes_accessed=600000, transcendentals=0),
        compiler_params=room(),
        **kw,
    )(owners, subs, counts, pair, visibility, coordinate)


def block_transpose(rows):
    lane = lax.broadcasted_iota(jnp.int32, (8, LANES), 1)
    rows = list(rows)
    for bit in range(2):
        step = SIDE << bit
        upper = (lane & step) != 0
        for low in range(4):
            if low >> bit & 1:
                continue
            high = low | 1 << bit
            x, y = rows[low], rows[high]
            rows[low] = jnp.where(upper, pltpu.roll(y, step, 1), x)
            rows[high] = jnp.where(upper, y, pltpu.roll(x, LANES - step, 1))
    return rows


BATCH = 4


def grid_kernel(meta, offs, rows_ref, x_ref, acc, coords, order, bucket):
    acc[...] = jnp.zeros_like(acc)
    for t in range(PEERS):
        coords[t] = rows_ref[t, ROWS - 16:ROWS, :].astype(F32)

    def gather(t, carry):
        count, spare = carry
        for k in range(PER):
            b = t * PER + k
            sub = meta[t * META + 2 * k]
            live = meta[t * META + 2 * k + 1]
            order[count] = b
            bucket[count] = (k // CAP) * SUBS + sub
            spare = jnp.where(live == 0, b, spare)
            count = count + live
        return count, spare

    count, spare = lax.fori_loop(0, PEERS, gather, (jnp.int32(0), jnp.int32(0)))
    for j in range(BATCH):
        order[count + j] = spare
        bucket[count + j] = 0

    sublane = lax.broadcasted_iota(jnp.int32, (8, LANES), 0).astype(F32)
    seed_l = (sublane * 4.0 - 16.0) * (1.0 / SIDE)
    seed_m = (sublane - 16.0) * (1.0 / SIDE)

    @pl.loop(0, (count + (BATCH - 1)) // BATCH)
    def _(step):
        for j in range(BATCH):
            b = order[step * BATCH + j]
            key = bucket[step * BATCH + j]
            sub = key % SUBS
            t = b // PER
            k = b % PER
            tile = rows_ref[t, pl.ds(pl.multiple_of(k // CAP * 16, 16), 16), :].astype(F32)
            tile = jnp.where(k % CAP == 0, tile[0:8], tile[8:16])
            u = coords[t, pl.ds(U_ROW - (ROWS - 16) + k, 1), :]
            v = coords[t, pl.ds(V_ROW - (ROWS - 16) + k, 1), :]
            du = jnp.broadcast_to(u - offs[0, 0, sub].astype(F32), (8, LANES))
            dv = jnp.broadcast_to(v - offs[0, 1, sub].astype(F32), (8, LANES))
            turn_l = cis(du * (1.0 / SIDE))
            turn_m = cis(dv * (8.0 / SIDE))
            current = cis(du * seed_l)
            cos_rows, sin_rows = [current[0]], [current[1]]
            for _ in range(3):
                current = times(current, turn_l)
                cos_rows.append(current[0])
                sin_rows.append(current[1])
            left = jnp.concatenate(cos_rows + sin_rows, axis=0).astype(BF16)
            phase = [cis(dv * seed_m)]
            for _ in range(3):
                phase.append(times(phase[-1], turn_m))
            real_rows, imag_rows = [], []
            for p in range(4):
                vis = tile[p:p + 1, :], tile[4 + p:5 + p, :]
                for m in range(4):
                    real, imag = times(vis, phase[m])
                    real_rows.append(real)
                    imag_rows.append(imag)
            right = jnp.concatenate(real_rows + imag_rows, axis=0).astype(BF16)
            acc[key] += lax.dot_general(
                left, right, (((1,), (1,)), ((), ())), preferred_element_type=F32
            )

    @pl.loop(0, SLOTS * SUBS)
    def _(key):
        upper = acc[key, 0:SIDE, :]
        lower = acc[key, SIDE:2 * SIDE, :]
        real = upper[:, :LANES] - lower[:, LANES:]
        imag = upper[:, LANES:] + lower[:, :LANES]
        for part, image in enumerate((real, imag)):
            for p, plane in enumerate(block_transpose([image[8 * b:8 * b + 8] for b in range(4)])):
                x_ref[key, 4 * part + p] = plane


def grid_blocks(meta, offs, rows, **kw):
    return pl.pallas_call(
        grid_kernel,
        out_shape=jax.ShapeDtypeStruct((SLOTS * SUBS, 8, 8, LANES), F32),
        in_specs=[smem(), smem(), vmem()],
        out_specs=vmem(),
        scratch_shapes=[
            pltpu.VMEM((SLOTS * SUBS, 2 * SIDE, 8 * SIDE), F32),
            pltpu.VMEM((PEERS, 16, LANES), F32),
            pltpu.SMEM((PEERS * PER + BATCH,), jnp.int32),
            pltpu.SMEM((PEERS * PER + BATCH,), jnp.int32),
        ],
        name="grid_blocks",
        cost_estimate=pl.CostEstimate(flops=800000000, bytes_accessed=800000, transcendentals=0),
        compiler_params=room(),
        **kw,
    )(meta, offs, rows)


COPIES = 4


def chunk_kernel(screens_ref, out_ref, in_ref, arrived):
    t = lax.axis_index("tm")
    lanes = pl.ds(pl.multiple_of(t // 2 * LANES, LANES), LANES)
    share = STATIONS // COPIES
    copies = []
    for c in range(COPIES):
        some = pl.ds(c * share, share)
        copies.append(pltpu.make_async_copy(screens_ref.at[0, some, :, lanes], in_ref.at[some], arrived.at[c]))
        copies[-1].start()
    odd = t % 2 == 1
    low = lax.broadcasted_iota(jnp.int32, (8, LANES), 0) < 4

    def two(first, second):
        a, b = in_ref[first].astype(F32), in_ref[second].astype(F32)
        a, b = jnp.where(odd, pltpu.roll(a, 4, 0), a), jnp.where(odd, b, pltpu.roll(b, 4, 0))
        return jnp.where(low, a, b)

    for j in range(NEAR):
        first = j * ST_PIECE
        if first % share == 0:
            copies[first // share].wait()
        out_ref[j] = jnp.concatenate([two(first, first + 1), two(first + 2, first + 3)], axis=0).astype(BF16)


def chunk_of(screens, **kw):
    return pl.pallas_call(
        chunk_kernel,
        out_shape=jax.ShapeDtypeStruct((NEAR, ST_PIECE * 4, LANES), BF16),
        in_specs=[pl.BlockSpec(memory_space=pltpu.HBM)],
        out_specs=vmem(),
        scratch_shapes=[pltpu.VMEM((STATIONS, 8, LANES), BF16), pltpu.SemaphoreType.DMA((COPIES,))],
        name="cut_chunk",
        **kw,
    )(screens)


def pick_near_kernel(roots, in_ref, out_ref):
    for s in range(SLOTS):
        out_ref[s] = in_ref[roots[s] // FAR]


def pick_near(roots, pieces, **kw):
    return pl.pallas_call(
        pick_near_kernel,
        out_shape=jax.ShapeDtypeStruct((SLOTS, 16, LANES), BF16),
        in_specs=[smem(), vmem()],
        out_specs=vmem(),
        name="pick_near",
        compiler_params=room(),
        **kw,
    )(roots, pieces)


def pick_far_kernel(roots, *refs):
    out_ref = refs[FAR]
    me = lax.axis_index("uv")
    pieces = []
    for s in range(SLOTS):
        shift = (me - roots[s] + FAR * NEAR) % FAR
        piece = refs[0][s].astype(F32)
        for k in range(1, FAR):
            piece = jnp.where(shift == k, refs[k][s].astype(F32), piece)
        pieces.append(piece)
    rows = jnp.concatenate(
        [pieces[s][4 * i:4 * i + 4] for i in range(ST_PIECE) for s in range(SLOTS)], axis=0
    ).astype(BF16)
    for j in range(NEAR):
        out_ref[j] = rows


def pick_far(roots, pieces, **kw):
    return pl.pallas_call(
        pick_far_kernel,
        out_shape=jax.ShapeDtypeStruct((NEAR, ST_PIECE * SLOTS * 4, LANES), BF16),
        in_specs=[smem()] + [vmem()] * FAR,
        out_specs=vmem(),
        name="pick_far",
        cost_estimate=pl.CostEstimate(flops=5200000000, bytes_accessed=800000, transcendentals=0),
        compiler_params=room(),
        **kw,
    )(roots, *pieces)


ROWS_ST = SLOTS * 4


def asked_kernel(meta, in_ref, out_ref, table, stage):
    for z in range(NEAR):
        wide = in_ref[z].astype(F32)
        for i in range(ST_PIECE):
            table[z * ST_PIECE + i, 0:ROWS_ST, :] = wide[ROWS_ST * i:ROWS_ST * (i + 1)]

    @pl.loop(0, PEERS)
    def _(t):
        for r in range(REQS):
            station = meta[t * META + PAIR_LANE + r]
            stage[ROWS_ST * r:ROWS_ST * (r + 1), :] = table[station, 0:ROWS_ST, :]
        out_ref[t] = stage[...].astype(BF16)


def asked(meta, pieces, **kw):
    return pl.pallas_call(
        asked_kernel,
        out_shape=jax.ShapeDtypeStruct((PEERS, REQS * ROWS_ST, LANES), BF16),
        in_specs=[smem(), vmem()],
        out_specs=vmem(),
        scratch_shapes=[
            pltpu.VMEM((STATIONS, 16, LANES), F32),
            pltpu.VMEM((REQS * ROWS_ST, LANES), F32),
        ],
        name="asked_stations",
        cost_estimate=pl.CostEstimate(flops=1000000, bytes_accessed=600000, transcendentals=0),
        compiler_params=room(),
        **kw,
    )(meta, pieces)


def screen_kernel(x_ref, in_ref, out_ref, wide, tmp):
    rows = REQS * ROWS_ST
    for t in range(PEERS):
        wide[rows * t:rows * (t + 1), :] = in_ref[t].astype(F32)

    def entry(request, slot, p, half):
        start = half * rows + request * ROWS_ST + slot * 4 + p
        return wide[pl.ds(start, 8, stride=2 * rows), :]

    def product(first, second):
        result = []
        for i in range(2):
            for j in range(2):
                one = times(first[2 * i], second[j])
                two = times(first[2 * i + 1], second[2 + j])
                result.append((one[0] + two[0], one[1] + two[1]))
        return result

    for sub in range(SUBS):
        total = None
        for slot in range(SLOTS):
            first = [(entry(2 * sub, slot, p, 0), entry(2 * sub, slot, p, 1)) for p in range(4)]
            second = [(entry(2 * sub + 1, slot, p, 0), -entry(2 * sub + 1, slot, p, 1)) for p in (0, 2, 1, 3)]
            key = slot * SUBS + sub
            image = [(x_ref[key, p], x_ref[key, 4 + p]) for p in range(4)]
            part = product(product(first, image), second)
            if total is None:
                total = part
            else:
                total = [(a[0] + b[0], a[1] + b[1]) for a, b in zip(total, part)]
        for p in range(4):
            tmp[8 * p:8 * p + 8, :] = total[p][0]
            tmp[32 + 8 * p:40 + 8 * p, :] = total[p][1]
        for a in range(8):
            out_ref[0, sub, :, LANES * a:LANES * (a + 1)] = tmp[pl.ds(a, 8, stride=8), :]


def screen_product(x, screens, **kw):
    return pl.pallas_call(
        screen_kernel,
        out_shape=jax.ShapeDtypeStruct((1, SUBS, 8, SIDE * SIDE), F32),
        in_specs=[vmem(), vmem()],
        out_specs=vmem(),
        scratch_shapes=[
            pltpu.VMEM((PEERS * REQS * ROWS_ST, LANES), F32),
            pltpu.VMEM((64, LANES), F32),
        ],
        name="screen_product",
        cost_estimate=pl.CostEstimate(flops=3000000, bytes_accessed=1000000, transcendentals=0),
        compiler_params=room(),
        **kw,
    )(x, screens)


def meta_of(arrived):
    return arrived[:, META_ROW, :META].astype(jnp.int32).reshape(-1)


def on_device(visibility, coordinate, block_count, owner_index, subgrid_index, offsets,
              station_pair, screens, slot_owner):
    near = [[k * FAR + j for k in range(NEAR)] for j in range(FAR)]

    def shifted(array, shift):
        pairs = [(k * FAR + j, k * FAR + (j + shift) % FAR) for k in range(NEAR) for j in range(FAR)]
        return lax.ppermute(array, "uv", pairs)

    def exchange(array, axis, groups=None):
        return lax.all_to_all(array, axis, 0, 0, axis_index_groups=groups, tiled=True)

    pieces = exchange(chunk_of(screens), "uv", near)
    sent = pack(owner_index[..., 0], subgrid_index, block_count, station_pair.swapaxes(1, 2), visibility, coordinate)
    pieces, sent = lax.optimization_barrier((pieces, sent))
    piece = pick_near(slot_owner, pieces)
    far = [piece] + [shifted(piece, shift) for shift in range(1, FAR)]
    arrived = exchange(sent, "tm")
    meta = meta_of(arrived)
    pieces = exchange(pick_far(slot_owner, far), "uv", near)
    x = grid_blocks(meta, offsets.swapaxes(1, 2), arrived)
    meta, x = lax.optimization_barrier((meta, x))
    wanted = exchange(asked(meta, pieces), "tm")
    return screen_product(x, wanted)


def solution(mesh):
    placed = (
        P(None, "uv", "tm", None, None),
        P(None, "uv", "tm", None, None),
        P(None, "uv", "tm"),
        P(None, "uv", "tm", None),
        P(None, "uv", "tm"),
        P("uv", "tm", None),
        P("uv", "tm", None),
        P("uv", None, None, None),
        P(),
    )
    return jax.shard_map(
        on_device, mesh=mesh, in_specs=placed, out_specs=P("uv", "tm", None, None), check_vma=False
    )
```
